256 devices in a mesh: seq: 128 (over y_lo, z, x, core), ch: 2 (over y_hi).
Axes of the slice: x: 4, y: 4 (y_hi: 2, y_lo: 2; y = y_hi * 2 + y_lo), z: 8, core: 2. Of those that a mesh axis runs over, the one named last changes fastest.
Arguments:
- stream: bfloat16 [2, 8192, 1024], P(None, 'seq', 'ch'), may hold values from -6 to 6
- skip: bfloat16 [2, 32768, 512], P(None, 'seq', 'ch'), may hold values from -6 to 6
- norm_gain: float32 [2, 1024], replicated, may hold values from 0.1 to 1.9
- norm_shift: float32 [2, 1024], replicated, may hold values from -3 to 3
- conv_weight: bfloat16 [2, 3, 1024, 512], P(None, None, None, 'ch'), may hold values from -0.109375 to 0.109375
- mid_gain: float32 [2, 512], P(None, 'ch'), may hold values from 0.1 to 1.9
- mid_shift: float32 [2, 512], P(None, 'ch'), may hold values from -3 to 3
- mix_weight: bfloat16 [2, 512, 1024], P(None, 'ch'), may hold values from -0.25 to 0.25
- up_gain: float32 [1024], replicated, may hold values from 0.1 to 1.9
- up_shift: float32 [1024], replicated, may hold values from -3 to 3
- up_weight: bfloat16 [8, 1024, 512], P(None, None, 'ch'), may hold values from -0.125 to 0.125
Outputs:
- upsampled: bfloat16 [2, 32768, 512], P(None, 'seq', 'ch')
The draws below stay inside these ranges and needn't reach their ends.
All inputs are finite; a program needn't handle non-finite values.
Results may differ from the reference program's by a relative error of at most 0.019.
Values may be sent and summed in bfloat16 or wider, within the bound.
A program may use at most 64 MiB of HBM per device.

```python
import jax
import jax.numpy as jnp
from jax import lax

C = 1024
H = 512
S = 512
RESIDUAL_LAYERS = 2
BATCH = 2
FINAL_SPACING = 64
LENGTH = 8192
OUT_LEN = 32768
N_CH = 2


def steps_of(stream_key, extent, pieces, low, largest):
    gain, own = 1.0, jax.random.fold_in(stream_key, 6)
    for position, parts in pieces:
        steps = jnp.exp(jax.random.uniform(jax.random.fold_in(own, position), (parts,), jnp.float32, low / len(pieces), largest / len(pieces)))
        gain = gain * jnp.repeat(steps, extent[position] // parts).reshape([-1 if axis == position else 1 for axis in range(len(extent))])
    return gain


def gaussian(rng, extent, deviation, reach, pieces=(), kind=jnp.bfloat16):
    loudness = steps_of(rng, extent, pieces, -0.22, 0.18) if pieces else 1.0
    array = jax.random.normal(rng, extent, jnp.float32) * deviation * loudness
    return jnp.minimum(jnp.maximum(array, -reach), reach).astype(kind)


def setup_inputs(seed: int = 0) -> dict:
    streams_of = jax.random.split(jax.random.key(seed), 12)
    stream = gaussian(streams_of[0], (BATCH, LENGTH, C), 1.0, 6.0, ((1, 128), (2, 2)))
    skip = gaussian(streams_of[1], (BATCH, OUT_LEN, S), 1.0, 6.0, ((1, 128), (2, 2)))
    norm_gain = jnp.clip(1.0 + 0.18 * jax.random.normal(streams_of[2], (RESIDUAL_LAYERS, C), jnp.float32), 0.1, 1.9)
    norm_shift = gaussian(streams_of[3], (RESIDUAL_LAYERS, C), 0.5, 3.0, (), jnp.float32)
    conv_weight = gaussian(streams_of[4], (RESIDUAL_LAYERS, 3, C, H), (3 * C) ** -0.5, 0.109375, ((3, 2),))
    mid_gain = jnp.clip(1.0 + 0.18 * jax.random.normal(streams_of[5], (RESIDUAL_LAYERS, H), jnp.float32), 0.1, 1.9)
    mid_shift = gaussian(streams_of[6], (RESIDUAL_LAYERS, H), 0.5, 3.0, ((1, 2),), jnp.float32)
    mix_weight = gaussian(streams_of[7], (RESIDUAL_LAYERS, H, C), H ** -0.5, 0.25, ((1, 2),))
    up_gain = jnp.clip(1.0 + 0.18 * jax.random.normal(streams_of[8], (C,), jnp.float32), 0.1, 1.9)
    up_shift = gaussian(streams_of[9], (C,), 0.5, 3.0, (), jnp.float32)
    up_weight = gaussian(streams_of[10], (8, C, S), (2 * C) ** -0.5, 0.125, ((2, 2),))
    return dict(stream=stream, skip=skip, norm_gain=norm_gain, norm_shift=norm_shift, conv_weight=conv_weight, mid_gain=mid_gain, mid_shift=mid_shift, mix_weight=mix_weight, up_gain=up_gain, up_shift=up_shift, up_weight=up_weight)


def gelu_act(values):
    return jax.nn.gelu(values)


def reference(stream, skip, norm_gain, norm_shift, conv_weight, mid_gain, mid_shift, mix_weight, up_gain, up_shift, up_weight):
    seq_count, length, width = stream.shape
    inner = conv_weight.shape[3]
    stream_now = stream
    for layer_number in range(RESIDUAL_LAYERS):
        tap_spacing = FINAL_SPACING // 2 ** (RESIDUAL_LAYERS - 1 - layer_number)
        activated = gelu_act(stream_now.astype(jnp.float32) * norm_gain[layer_number] + norm_shift[layer_number]).astype(jnp.bfloat16)
        padded = jnp.pad(activated, ((0, 0), (tap_spacing, tap_spacing), (0, 0)))
        conv_out = jnp.zeros((seq_count * length, inner), jnp.float32)
        for tap_index in range(3):
            receptive_span = padded[:, tap_index * tap_spacing:tap_index * tap_spacing + length].reshape(-1, width)
            conv_out = conv_out + jnp.dot(receptive_span, conv_weight[layer_number, tap_index], preferred_element_type=jnp.float32)
        hidden = gelu_act(conv_out * mid_gain[layer_number] + mid_shift[layer_number]).astype(jnp.bfloat16)
        half_width = inner // N_CH
        residual_delta = jnp.zeros((seq_count * length, width), jnp.float32)
        for part_index in range(N_CH):
            contrib = jnp.dot(hidden[:, part_index * half_width:(part_index + 1) * half_width], mix_weight[layer_number, part_index * half_width:(part_index + 1) * half_width], preferred_element_type=jnp.float32).astype(jnp.bfloat16)
            contrib = lax.optimization_barrier(contrib)
            residual_delta = residual_delta + contrib.astype(jnp.float32)
        stream_now = (stream_now.astype(jnp.float32) + residual_delta.reshape(seq_count, length, width)).astype(jnp.bfloat16)
    coarse = gelu_act(stream_now.astype(jnp.float32) * up_gain + up_shift).astype(jnp.bfloat16)
    out_width = up_weight.shape[2]
    centre_kernel = jnp.transpose(up_weight[2:6], (1, 0, 2)).reshape(width, 4 * out_width)
    early_kernel = jnp.transpose(up_weight[6:8], (1, 0, 2)).reshape(width, 2 * out_width)
    late_kernel = jnp.transpose(up_weight[0:2], (1, 0, 2)).reshape(width, 2 * out_width)

    def one_sequence(batch_pair):
        coarse_row, skip_row = batch_pair
        centre = jnp.dot(coarse_row, centre_kernel, preferred_element_type=jnp.float32).reshape(length, 4, out_width)
        prior_state = jnp.pad(coarse_row, ((1, 0), (0, 0)))[:-1]
        following = jnp.pad(coarse_row, ((0, 1), (0, 0)))[1:]
        from_prev = jnp.dot(prior_state, early_kernel, preferred_element_type=jnp.float32).reshape(length, 2, out_width)
        from_next = jnp.dot(following, late_kernel, preferred_element_type=jnp.float32).reshape(length, 2, out_width)
        combined = centre + jnp.concatenate([from_prev, from_next], axis=1) + skip_row.reshape(length, 4, out_width).astype(jnp.float32)
        return combined.reshape(4 * length, out_width).astype(jnp.bfloat16)

    return lax.map(one_sequence, (coarse, skip))
```

```python
import functools

import jax
import jax.numpy as jnp
from jax import lax
from jax.experimental import pallas as pl
from jax.experimental.pallas import tpu as pltpu
from jax.sharding import PartitionSpec as P

MESH = pl.DeviceIdType.MESH
F32 = jnp.float32
BF16 = jnp.bfloat16
ROWS = 64
GELU_A = 0.7978845608028654
GELU_B = 0.7978845608028654 * 0.044715


def gelu(v):
    half = 0.5 * v
    return half + half * jnp.tanh(v * (GELU_A + GELU_B * (v * v)))


def dot(a, b):
    return jnp.dot(a, b, preferred_element_type=F32)


def kernel(
    seq_devices,
    stream, skip, norm_gain, norm_shift, conv_weight, mid_gain, mid_shift, mix_weight, up_gain, up_shift, up_weight,
    out,
    xr, a0, hb, mw, cw, uw, a1, x1, h1, eh, uf, outf, outb, skipb, ng, ns, mg, ms, ug, us,
    local_sem, send_sem, recv_sem,
):
    s = lax.axis_index("seq")
    g = lax.axis_index("ch")
    core = lax.rem(s, 2)
    o = 1 - g
    sib_s = s + 1 - 2 * core
    crs_s = lax.rem(s + seq_devices - 1 + 2 * core, seq_devices)
    cut_s = lax.rem(s + seq_devices // 2, seq_devices)
    par = {"seq": s, "ch": o}
    sib = {"seq": sib_s, "ch": g}
    crs = {"seq": crs_s, "ch": g}
    dcr = {"seq": crs_s, "ch": o}
    dsb = {"seq": sib_s, "ch": o}
    cut = {"seq": cut_s, "ch": o}
    partners = (par, sib, crs, dcr, dsb, cut)

    barrier = pltpu.get_barrier_semaphore()
    for device in partners:
        pl.semaphore_signal(barrier, inc=1, device_id=device, device_id_type=MESH)

    local = []

    def fetch(src, dst):
        copy = pltpu.make_async_copy(src, dst, local_sem.at[len(local)])
        copy.start()
        local.append(copy)
        return copy

    own_copy = fetch(stream, xr.at[g, 1])
    gain_copies = [
        fetch(norm_gain, ng), fetch(norm_shift, ns), fetch(mid_gain, mg), fetch(mid_shift, ms),
    ]
    cw0_copy = fetch(conv_weight.at[0], cw.at[0])
    mw0_copy = fetch(mix_weight.at[0], mw.at[0, g])
    cw1_copy = fetch(conv_weight.at[1], cw.at[1])
    mw1_copy = fetch(mix_weight.at[1], mw.at[1, g])
    up_copies = [fetch(up_gain, ug), fetch(up_shift, us), fetch(up_weight, uw), fetch(skip, skipb)]

    sends = []

    def send(src, dst, device):
        index = len(sends)
        copy = pltpu.make_async_remote_copy(
            src_ref=src, dst_ref=dst, send_sem=send_sem.at[index], recv_sem=recv_sem.at[index],
            device_id=device, device_id_type=MESH,
        )
        copy.start()
        sends.append(copy)
        return copy

    to_sib = 2 * core
    to_crs = 2 - 2 * core
    my_sib = 2 - 2 * core
    my_crs = 2 * core
    near = pl.ds(pl.multiple_of(32 * core, 32), 32)
    far = pl.ds(pl.multiple_of(32 - 32 * core, 32), 32)

    pl.semaphore_wait(barrier, len(partners))
    x_par = send(stream, xr.at[g, 1], par)
    x_dcr = send(stream.at[:, near], xr.at[g, to_crs, :, near], dcr)
    x_crs = send(stream.at[:, near], xr.at[g, to_crs, :, near], crs)
    x_sib = send(stream, xr.at[g, to_sib], sib)
    x_dcr2 = send(stream.at[:, far], xr.at[g, to_crs, :, far], dcr)
    x_crs2 = send(stream.at[:, far], xr.at[g, to_crs, :, far], crs)
    mine = pl.ds(pl.multiple_of(128 * core, 128), 128)
    w_cut = [send(mix_weight.at[0, mine], mw.at[0, g, mine], cut)]

    crs_valid = jnp.where(jnp.logical_and(s > 0, s < seq_devices - 1), 1.0, 0.0).astype(F32)
    left_valid = jnp.where(s > 0, 1.0, 0.0).astype(F32)
    right_valid = jnp.where(s < seq_devices - 1, 1.0, 0.0).astype(F32)

    def activate0(gg, slot, rows, dst_row, valid):
        cols = pl.ds(pl.multiple_of(gg * 512, 512), 512)
        gain = ng[0:1, cols]
        shift = ns[0:1, cols]
        for b in range(2):
            v = gelu(xr[gg, slot, b, rows, :].astype(F32) * gain + shift)
            if valid is not None:
                v = v * valid
            a0[gg, b, dst_row, :] = v.astype(BF16)

    def conv0(gg):
        acc = None
        for k in range(3):
            term = dot(
                a0[gg, :, 32 * k : 32 * k + ROWS, :].reshape(128, 512),
                cw[0, k, pl.ds(pl.multiple_of(gg * 512, 512), 512), :],
            )
            acc = term if acc is None else acc + term
        return acc

    sib_src = pl.ds(pl.multiple_of(32 * core, 32), 32)
    crs_src = pl.ds(pl.multiple_of(32 - 32 * core, 32), 32)
    sib_dst = pl.ds(pl.multiple_of(96 - 96 * core, 32), 32)
    crs_dst = pl.ds(pl.multiple_of(96 * core, 32), 32)
    whole = pl.ds(0, ROWS)
    centre = pl.ds(32, ROWS)

    own_copy.wait()
    for copy in gain_copies:
        copy.wait()
    activate0(g, 1, whole, centre, None)
    x_sib.wait_recv()
    activate0(g, my_sib, sib_src, sib_dst, None)
    x_crs.wait_recv()
    activate0(g, my_crs, crs_src, crs_dst, crs_valid)
    cw0_copy.wait()
    acc = conv0(g)
    x_par.wait_recv()
    x_fwd = send(xr.at[o, 1], xr.at[o, to_sib], sib)
    activate0(o, 1, whole, centre, None)
    x_dcr.wait_recv()
    activate0(o, my_crs, crs_src, crs_dst, crs_valid)
    x_fwd.wait_recv()
    activate0(o, my_sib, sib_src, sib_dst, None)
    acc = acc + conv0(o)
    hb[g, 1] = gelu(acc * mg[0:1, :] + ms[0:1, :]).astype(BF16)

    h_par = send(hb.at[g, 1], hb.at[g, 1], par)
    h_dcr = send(hb.at[g, 1], hb.at[g, to_crs], dcr)
    h_crs = send(hb.at[g, 1], hb.at[g, to_crs], crs)
    h_sib = send(hb.at[g, 1], hb.at[g, to_sib], sib)
    w_cut.append(send(mix_weight.at[1, mine], mw.at[1, g, mine], cut))
    w_cut[0].wait_recv()
    w_fwd = [send(mw.at[0, o, mine], mw.at[0, o, mine], sib)]

    def mix0(slot, valid):
        for n in range(4):
            cols = slice(256 * n, 256 * n + 256)
            gg, inner = n // 2, slice(256 * (n % 2), 256 * (n % 2) + 256)
            z = dot(hb[0, slot], mw[0, 0, :, cols]) + dot(hb[1, slot], mw[0, 1, :, cols])
            x = xr[gg, slot, :, :, inner].reshape(128, 256).astype(F32) + z
            x = x.astype(BF16)
            x1[slot, :, cols] = x
            v = gelu(x.astype(F32) * ng[1:2, cols] + ns[1:2, cols])
            if valid is not None:
                v = v * valid
            a1[slot, :, cols] = v.astype(BF16)
        return dot(a1[slot], cw[1, slot])

    mw0_copy.wait()
    cw1_copy.wait()
    h_par.wait_recv()
    h_fwd = send(hb.at[o, 1], hb.at[o, to_sib], sib)
    w_fwd[0].wait_recv()
    acc = mix0(1, None)
    h_sib.wait_recv()
    h_fwd.wait_recv()
    acc = acc + mix0(my_sib, None)
    x_crs2.wait_recv()
    x_dcr2.wait_recv()
    h_crs.wait_recv()
    h_dcr.wait_recv()
    acc = acc + mix0(my_crs, crs_valid)
    h1[g] = gelu(acc * mg[1:2, :] + ms[1:2, :]).astype(BF16).reshape(2, ROWS, 256)

    last = pl.ds(pl.multiple_of(48 - 48 * core, 16), 16)
    first = pl.ds(pl.multiple_of(48 * core, 16), 16)
    g_par = send(h1.at[g], h1.at[g], par)
    g_dcr = send(h1.at[g, :, first], eh.at[g, 1 - core], dcr)
    g_crs = send(h1.at[g, :, first], eh.at[g, 1 - core], crs)
    g_dsb = send(h1.at[g, :, last], eh.at[g, core], dsb)
    g_sib = send(h1.at[g, :, last], eh.at[g, core], sib)

    w_cut[1].wait_recv()
    w_fwd.append(send(mw.at[1, o, mine], mw.at[1, o, mine], sib))
    mw1_copy.wait()
    for copy in up_copies:
        copy.wait()
    w_fwd[1].wait_recv()

    def top(h_pair, base, cols):
        z = dot(h_pair[0], mw[1, 0, :, cols]) + dot(h_pair[1], mw[1, 1, :, cols])
        x = (base.astype(F32) + z).astype(BF16).astype(F32)
        v = gelu(x * ug[0:1, cols] + us[0:1, cols])
        return v.astype(BF16).astype(F32)

    g_par.wait_recv()
    for n in range(4):
        cols = slice(256 * n, 256 * n + 256)
        u = top([h1[0].reshape(128, 256), h1[1].reshape(128, 256)], x1[1, :, cols], cols)
        for b in range(2):
            uf[b, 8 : 8 + ROWS, cols] = u[ROWS * b : ROWS * b + ROWS]
    for copy in (g_sib, g_crs, g_dsb, g_dcr):
        copy.wait_recv()
    for n in range(4):
        cols = slice(256 * n, 256 * n + 256)
        for side in range(2):
            first_row = 48 if side == 0 else 0
            base = jnp.concatenate(
                [x1[2 * side, ROWS * b + first_row : ROWS * b + first_row + 16, cols] for b in range(2)], axis=0
            )
            u = top([eh[0, side].reshape(32, 256), eh[1, side].reshape(32, 256)], base, cols)
            u = u * (left_valid if side == 0 else right_valid)
            for b in range(2):
                if side == 0:
                    uf[b, 0:8, cols] = u[16 * b + 8 : 16 * b + 16]
                else:
                    uf[b, 8 + ROWS : 16 + ROWS, cols] = u[16 * b : 16 * b + 8]

    def rows_at(offset):
        return jnp.concatenate(
            [uf[b, 8 + offset : 8 + offset + ROWS, :].astype(BF16) for b in range(2)], axis=0
        )

    here, before, after = rows_at(0), rows_at(-1), rows_at(1)
    for r in range(4):
        if r < 2:
            v = dot(here, uw[2 + r]) + dot(before, uw[6 + r])
        else:
            v = dot(here, uw[2 + r]) + dot(after, uw[r - 2])
        for b in range(2):
            for half in range(2):
                outf[b, half, pl.ds(r, ROWS, stride=4), :] = v[
                    ROWS * b : ROWS * b + ROWS, 128 * half : 128 * half + 128
                ]
    for half in range(2):
        lanes = slice(128 * half, 128 * half + 128)
        outb[:, :, lanes] = (outf[:, half] + skipb[:, :, lanes].astype(F32)).astype(BF16)
    out_copy = pltpu.make_async_copy(outb, out, local_sem.at[len(local)])
    out_copy.start()
    for copy in sends:
        copy.wait_send()
    out_copy.wait()


def body(
    seq_devices, stream, skip, norm_gain, norm_shift, conv_weight, mid_gain, mid_shift, mix_weight, up_gain, up_shift, up_weight
):
    anywhere = pl.BlockSpec(memory_space=pl.ANY)
    return pl.pallas_call(
        functools.partial(kernel, seq_devices),
        name="bottleneck",
        out_shape=jax.ShapeDtypeStruct((2, 256, 256), BF16),
        in_specs=[anywhere] * 11,
        out_specs=anywhere,
        scratch_shapes=[
            pltpu.VMEM((2, 3, 2, 64, 512), BF16),
            pltpu.VMEM((2, 2, 128, 512), BF16),
            pltpu.VMEM((2, 3, 128, 256), BF16),
            pltpu.VMEM((2, 2, 256, 1024), BF16),
            pltpu.VMEM((2, 3, 1024, 256), BF16),
            pltpu.VMEM((8, 1024, 256), BF16),
            pltpu.VMEM((3, 128, 1024), BF16),
            pltpu.VMEM((3, 128, 1024), BF16),
            pltpu.VMEM((2, 2, 64, 256), BF16),
            pltpu.VMEM((2, 2, 2, 16, 256), BF16),
            pltpu.VMEM((2, 80, 1024), F32),
            pltpu.VMEM((2, 2, 256, 128), F32),
            pltpu.VMEM((2, 256, 256), BF16),
            pltpu.VMEM((2, 256, 256), BF16),
            pltpu.VMEM((2, 1024), F32),
            pltpu.VMEM((2, 1024), F32),
            pltpu.VMEM((2, 256), F32),
            pltpu.VMEM((2, 256), F32),
            pltpu.VMEM((1, 1024), F32),
            pltpu.VMEM((1, 1024), F32),
            pltpu.SemaphoreType.DMA((16,)),
            pltpu.SemaphoreType.DMA((24,)),
            pltpu.SemaphoreType.DMA((24,)),
        ],
        compiler_params=pltpu.CompilerParams(
            collective_id=0, has_side_effects=True, vmem_limit_bytes=63 * 1024 * 1024
        ),
    )(
        stream, skip, norm_gain, norm_shift, conv_weight, mid_gain, mid_shift, mix_weight,
        up_gain.reshape(1, -1), up_shift.reshape(1, -1), up_weight,
    )


def solution(mesh):
    placed = (
        P(None, "seq", "ch"),
        P(None, "seq", "ch"),
        P(),
        P(),
        P(None, None, None, "ch"),
        P(None, "ch"),
        P(None, "ch"),
        P(None, "ch", None),
        P(),
        P(),
        P(None, None, "ch"),
    )
    return jax.shard_map(
        functools.partial(body, mesh.shape["seq"]),
        mesh=mesh, in_specs=placed, out_specs=P(None, "seq", "ch"), check_vma=False,
    )
```

```python
import functools

import jax
import jax.numpy as jnp
from jax import lax
from jax.experimental import pallas as pl
from jax.experimental.pallas import tpu as pltpu
from jax.sharding import PartitionSpec as P

MESH = pl.DeviceIdType.MESH
F32 = jnp.float32
BF16 = jnp.bfloat16
ROWS = 64
GELU_A = 0.7978845608028654
GELU_B = 0.7978845608028654 * 0.044715


def gelu(v):
    half = 0.5 * v
    return half + half * jnp.tanh(v * (GELU_A + GELU_B * (v * v)))


def dot(a, b):
    return jnp.dot(a, b, preferred_element_type=F32)


def kernel(
    seq_devices,
    stream, skip, norm_gain, norm_shift, conv_weight, mid_gain, mid_shift, mix_weight, up_gain, up_shift, up_weight,
    out,
    xr, a0, hb, mw, cw, uw, a1, x1, h1, eh, uf, outf, skipb, ng, ns, mg, ms, ug, us,
    local_sem, send_sem, recv_sem,
):
    s = lax.axis_index("seq")
    g = lax.axis_index("ch")
    core = lax.rem(s, 2)
    o = 1 - g
    sib_s = s + 1 - 2 * core
    crs_s = lax.rem(s + seq_devices - 1 + 2 * core, seq_devices)
    cut_s = lax.rem(s + seq_devices // 2, seq_devices)
    x_bit = lax.rem(s // 2, 2)
    z_bit = lax.rem(s // 8, 2)
    x_step = 2 - 4 * x_bit
    z_step = 8 - 16 * z_bit
    has_crs = jnp.logical_and(s > 0, s < seq_devices - 1)
    par = {"seq": s, "ch": o}
    sib = {"seq": sib_s, "ch": g}
    crs = {"seq": crs_s, "ch": g}
    dcr = {"seq": crs_s, "ch": o}
    dsb = {"seq": sib_s, "ch": o}
    cut = {"seq": cut_s, "ch": o}
    mates = [{"seq": s + x_step, "ch": g}, {"seq": s + z_step, "ch": g}, {"seq": s + x_step + z_step, "ch": g}]
    partners = [par, sib, dsb, cut] + mates

    barrier = pltpu.get_barrier_semaphore()
    for device in partners:
        pl.semaphore_signal(barrier, inc=1, device_id=device, device_id_type=MESH)

    @pl.when(has_crs)
    def _():
        for device in (crs, dcr):
            pl.semaphore_signal(barrier, inc=1, device_id=device, device_id_type=MESH)

    local = []

    def fetch(src, dst):
        copy = pltpu.make_async_copy(src, dst, local_sem.at[len(local)])
        copy.start()
        local.append(copy)
        return copy

    own_copy = fetch(stream, xr.at[g, 1])
    gain_copies = [
        fetch(norm_gain, ng), fetch(norm_shift, ns), fetch(mid_gain, mg), fetch(mid_shift, ms),
    ]
    cw0_copy = fetch(conv_weight.at[0], cw.at[0])
    mw0_copy = fetch(mix_weight.at[0], mw.at[0, g])
    cw1_copy = fetch(conv_weight.at[1], cw.at[1])
    mw1_copy = fetch(mix_weight.at[1], mw.at[1, g])
    up_copies = [fetch(up_gain, ug), fetch(up_shift, us), fetch(up_weight, uw), fetch(skip, skipb)]

    sends = []

    def send(src, dst, device, when=None):
        index = len(sends)
        copy = pltpu.make_async_remote_copy(
            src_ref=src, dst_ref=dst, send_sem=send_sem.at[index], recv_sem=recv_sem.at[index],
            device_id=device, device_id_type=MESH,
        )
        sends.append((copy, when))
        if when is None:
            copy.start()
        else:
            pl.when(when)(copy.start)
        return copy

    def arrive(*copies):
        for copy in copies:
            copy.wait_recv()

    def arrive_crs(*copies):
        @pl.when(has_crs)
        def _():
            for copy in copies:
                copy.wait_recv()

    to_sib = 2 * core
    to_crs = 2 - 2 * core
    my_sib = 2 - 2 * core
    my_crs = 2 * core
    near = pl.ds(pl.multiple_of(32 * core, 32), 32)
    far = pl.ds(pl.multiple_of(32 - 32 * core, 32), 32)
    mine = pl.ds(pl.multiple_of(128 * core, 128), 128)
    eighth = pl.ds(pl.multiple_of(128 * core + 64 * z_bit + 32 * x_bit, 32), 32)

    own_copy.wait()
    pl.semaphore_wait(barrier, jnp.where(has_crs, len(partners) + 2, len(partners)))
    x_own = xr.at[g, 1]
    x_par = send(x_own, xr.at[g, 1], par)
    x_crs = send(xr.at[g, 1, :, near], xr.at[g, to_crs, :, near], crs, has_crs)
    x_dcr = send(xr.at[g, 1, :, near], xr.at[g, to_crs, :, near], dcr, has_crs)
    x_sib = send(x_own, xr.at[g, to_sib], sib)
    w_cut = [send(mix_weight.at[n, eighth], mw.at[n, g, eighth], cut) for n in range(2)]
    x_crs2 = send(xr.at[g, 1, :, far], xr.at[g, to_crs, :, far], crs, has_crs)


    def activate0(gg, slot, rows, dst_row, valid):
        cols = pl.ds(pl.multiple_of(gg * 512, 512), 512)
        gain = ng[0:1, cols]
        shift = ns[0:1, cols]
        for b in range(2):
            v = gelu(xr[gg, slot, b, rows, :].astype(F32) * gain + shift)
            if valid is not None:
                v = jnp.where(valid, v, 0.0)
            a0[gg, b, dst_row, :] = v.astype(BF16)

    def conv0(gg):
        acc = None
        for k in range(3):
            term = dot(
                a0[gg, :, 32 * k : 32 * k + ROWS, :].reshape(128, 512),
                cw[0, k, pl.ds(pl.multiple_of(gg * 512, 512), 512), :],
            )
            acc = term if acc is None else acc + term
        return acc

    sib_src = pl.ds(pl.multiple_of(32 * core, 32), 32)
    crs_src = pl.ds(pl.multiple_of(32 - 32 * core, 32), 32)
    sib_dst = pl.ds(pl.multiple_of(96 - 96 * core, 32), 32)
    crs_dst = pl.ds(pl.multiple_of(96 * core, 32), 32)
    whole = pl.ds(0, ROWS)
    centre = pl.ds(32, ROWS)

    for copy in gain_copies:
        copy.wait()
    activate0(g, 1, whole, centre, None)
    arrive(x_sib)
    activate0(g, my_sib, sib_src, sib_dst, None)
    arrive_crs(x_crs)
    activate0(g, my_crs, crs_src, crs_dst, has_crs)
    cw0_copy.wait()
    acc = conv0(g)
    arrive(x_par)
    x_fwd = send(xr.at[o, 1], xr.at[o, to_sib], sib)
    activate0(o, 1, whole, centre, None)
    arrive_crs(x_dcr)
    activate0(o, my_crs, crs_src, crs_dst, has_crs)
    arrive(w_cut[0])
    w_mate = [[send(mw.at[0, o, eighth], mw.at[0, o, eighth], mate) for mate in mates]]
    arrive(x_fwd)
    activate0(o, my_sib, sib_src, sib_dst, None)
    acc = acc + conv0(o)
    hb[g, 1] = gelu(acc * mg[0:1, :] + ms[0:1, :]).astype(BF16)

    h_own = hb.at[g, 1]
    h_par = send(h_own, hb.at[g, 1], par)
    h_crs = send(h_own, hb.at[g, to_crs], crs, has_crs)
    h_dcr = send(h_own, hb.at[g, to_crs], dcr, has_crs)
    h_sib = send(h_own, hb.at[g, to_sib], sib)
    x_rel = send(xr.at[o, 1, :, far], xr.at[o, to_crs, :, far], crs, has_crs)
    arrive(w_cut[1])
    w_mate.append([send(mw.at[1, o, eighth], mw.at[1, o, eighth], mate) for mate in mates])
    arrive(*w_mate[0])
    w_fwd = [send(mw.at[0, o, mine], mw.at[0, o, mine], sib)]

    def mix0(slot, valid):
        for n in range(4):
            cols = slice(256 * n, 256 * n + 256)
            gg, inner = n // 2, slice(256 * (n % 2), 256 * (n % 2) + 256)
            z = dot(hb[0, slot], mw[0, 0, :, cols]) + dot(hb[1, slot], mw[0, 1, :, cols])
            x = xr[gg, slot, :, :, inner].reshape(128, 256).astype(F32) + z
            x = x.astype(BF16)
            x1[slot, :, cols] = x
            v = gelu(x.astype(F32) * ng[1:2, cols] + ns[1:2, cols])
            if valid is not None:
                v = jnp.where(valid, v, 0.0)
            a1[slot, :, cols] = v.astype(BF16)
        return dot(a1[slot], cw[1, slot])

    mw0_copy.wait()
    cw1_copy.wait()
    arrive(h_par)
    h_fwd = send(hb.at[o, 1], hb.at[o, to_sib], sib)
    arrive(w_fwd[0])
    acc = mix0(1, None)
    arrive(h_sib)
    arrive(h_fwd)
    acc = acc + mix0(my_sib, None)
    arrive_crs(x_crs2)
    arrive_crs(x_rel)
    arrive_crs(h_crs)
    arrive_crs(h_dcr)
    acc = acc + mix0(my_crs, has_crs)
    h1[g] = gelu(acc * mg[1:2, :] + ms[1:2, :]).astype(BF16).reshape(2, ROWS, 256)

    last = pl.ds(pl.multiple_of(48 - 48 * core, 16), 16)
    first = pl.ds(pl.multiple_of(48 * core, 16), 16)
    g_par = send(h1.at[g], h1.at[g], par)
    g_crs = send(h1.at[g, :, first], eh.at[g, 1 - core], crs, has_crs)
    g_dcr = send(h1.at[g, :, first], eh.at[g, 1 - core], dcr, has_crs)
    g_dsb = send(h1.at[g, :, last], eh.at[g, core], dsb)
    g_sib = send(h1.at[g, :, last], eh.at[g, core], sib)

    arrive(*w_mate[1])
    w_fwd.append(send(mw.at[1, o, mine], mw.at[1, o, mine], sib))
    mw1_copy.wait()
    for copy in up_copies:
        copy.wait()
    arrive(w_fwd[1])

    def top(h_pair, base, cols):
        z = dot(h_pair[0], mw[1, 0, :, cols]) + dot(h_pair[1], mw[1, 1, :, cols])
        x = (base.astype(F32) + z).astype(BF16).astype(F32)
        v = gelu(x * ug[0:1, cols] + us[0:1, cols])
        return v.astype(BF16).astype(F32)

    arrive(g_par)
    for n in range(4):
        cols = slice(256 * n, 256 * n + 256)
        u = top([h1[0].reshape(128, 256), h1[1].reshape(128, 256)], x1[1, :, cols], cols)
        for b in range(2):
            uf[b, 8 : 8 + ROWS, cols] = u[ROWS * b : ROWS * b + ROWS]
    arrive(g_sib, g_dsb)
    arrive_crs(g_crs, g_dcr)
    for n in range(4):
        cols = slice(256 * n, 256 * n + 256)
        for side in range(2):
            first_row = 48 if side == 0 else 0
            base = jnp.concatenate(
                [x1[2 * side, ROWS * b + first_row : ROWS * b + first_row + 16, cols] for b in range(2)], axis=0
            )
            u = top([eh[0, side].reshape(32, 256), eh[1, side].reshape(32, 256)], base, cols)
            u = jnp.where(s > 0 if side == 0 else s < seq_devices - 1, u, 0.0)
            for b in range(2):
                if side == 0:
                    uf[b, 0:8, cols] = u[16 * b + 8 : 16 * b + 16]
                else:
                    uf[b, 8 + ROWS : 16 + ROWS, cols] = u[16 * b : 16 * b + 8]

    def rows_at(offset):
        return jnp.concatenate(
            [uf[b, 8 + offset : 8 + offset + ROWS, :].astype(BF16) for b in range(2)], axis=0
        )

    here, before, after = rows_at(0), rows_at(-1), rows_at(1)
    for r in range(4):
        if r < 2:
            v = dot(here, uw[2 + r]) + dot(before, uw[6 + r])
        else:
            v = dot(here, uw[2 + r]) + dot(after, uw[r - 2])
        for b in range(2):
            for half in range(2):
                outf[b, half, pl.ds(r, ROWS, stride=4), :] = v[
                    ROWS * b : ROWS * b + ROWS, 128 * half : 128 * half + 128
                ]
    for half in range(2):
        lanes = slice(128 * half, 128 * half + 128)
        out[:, :, lanes] = (outf[:, half] + skipb[:, :, lanes].astype(F32)).astype(BF16)
    for copy, when in sends:
        if when is None:
            copy.wait_send()
        else:
            pl.when(when)(copy.wait_send)


def body(
    seq_devices, stream, skip, norm_gain, norm_shift, conv_weight, mid_gain, mid_shift, mix_weight, up_gain, up_shift, up_weight
):
    anywhere = pl.BlockSpec(memory_space=pl.ANY)
    return pl.pallas_call(
        functools.partial(kernel, seq_devices),
        name="bottleneck",
        out_shape=pltpu.VMEM((2, 256, 256), BF16),
        in_specs=[anywhere] * 11,
        out_specs=pl.BlockSpec(memory_space=pltpu.VMEM),
        scratch_shapes=[
            pltpu.VMEM((2, 3, 2, 64, 512), BF16),
            pltpu.VMEM((2, 2, 128, 512), BF16),
            pltpu.VMEM((2, 3, 128, 256), BF16),
            pltpu.VMEM((2, 2, 256, 1024), BF16),
            pltpu.VMEM((2, 3, 1024, 256), BF16),
            pltpu.VMEM((8, 1024, 256), BF16),
            pltpu.VMEM((3, 128, 1024), BF16),
            pltpu.VMEM((3, 128, 1024), BF16),
            pltpu.VMEM((2, 2, 64, 256), BF16),
            pltpu.VMEM((2, 2, 2, 16, 256), BF16),
            pltpu.VMEM((2, 80, 1024), F32),
            pltpu.VMEM((2, 2, 256, 128), F32),
            pltpu.VMEM((2, 256, 256), BF16),
            pltpu.VMEM((2, 1024), F32),
            pltpu.VMEM((2, 1024), F32),
            pltpu.VMEM((2, 256), F32),
            pltpu.VMEM((2, 256), F32),
            pltpu.VMEM((1, 1024), F32),
            pltpu.VMEM((1, 1024), F32),
            pltpu.SemaphoreType.DMA((16,)),
            pltpu.SemaphoreType.DMA((32,)),
            pltpu.SemaphoreType.DMA((32,)),
        ],
        compiler_params=pltpu.CompilerParams(
            collective_id=0, has_side_effects=True, vmem_limit_bytes=56 * 1024 * 1024
        ),
    )(
        stream, skip, norm_gain, norm_shift, conv_weight, mid_gain, mid_shift, mix_weight,
        up_gain.reshape(1, -1), up_shift.reshape(1, -1), up_weight,
    )


def solution(mesh):
    placed = (
        P(None, "seq", "ch"),
        P(None, "seq", "ch"),
        P(),
        P(),
        P(None, None, None, "ch"),
        P(None, "ch"),
        P(None, "ch"),
        P(None, "ch", None),
        P(),
        P(),
        P(None, None, "ch"),
    )
    return jax.shard_map(
        functools.partial(body, mesh.shape["seq"]),
        mesh=mesh, in_specs=placed, out_specs=P(None, "seq", "ch"), check_vma=False,
    )
```

```python
import functools

import jax
import jax.numpy as jnp
from jax import lax
from jax.experimental import pallas as pl
from jax.experimental.pallas import tpu as pltpu
from jax.sharding import PartitionSpec as P

MESH = pl.DeviceIdType.MESH
F32 = jnp.float32
BF16 = jnp.bfloat16
ROWS = 64
GELU_A = 0.7978845608028654
GELU_B = 0.7978845608028654 * 0.044715


def gelu(v):
    half = 0.5 * v
    return half + half * jnp.tanh(v * (GELU_A + GELU_B * (v * v)))


def dot(a, b):
    return jnp.dot(a, b, preferred_element_type=F32)


def kernel(
    seq_devices,
    stream, skip, norm_gain, norm_shift, conv_weight, mid_gain, mid_shift, mix_weight, up_gain, up_shift, up_weight,
    out,
    xr, a0, hb, mw, cw, uw, a1, x1, h1, eh, uf, outf, zf, cf, accf, skipb, ng, ns, mg, ms, ug, us,
    local_sem, send_sem, recv_sem, go_sem,
):
    s = lax.axis_index("seq")
    g = lax.axis_index("ch")
    core = lax.rem(s, 2)
    o = 1 - g
    sib_s = s + 1 - 2 * core
    crs_s = lax.rem(s + seq_devices - 1 + 2 * core, seq_devices)
    cut_s = lax.rem(s + seq_devices // 2, seq_devices)
    x_at = lax.rem(s // 2, 4)
    z_bit = lax.rem(s // 8, 2)
    row = s - 2 * x_at
    x_next = row + 2 * lax.rem(x_at + 1, 4)
    x_last = row + 2 * lax.rem(x_at + 3, 4)
    z_step = 8 - 16 * z_bit
    y_bit = s // (seq_devices // 2)
    has_crs = jnp.logical_and(s > 0, s < seq_devices - 1)
    ahead = s == seq_devices // 2
    behind = s == seq_devices // 2 - 1
    turn = lax.rem(s, 8) == 7 * core
    at_once = jnp.logical_and(has_crs, jnp.logical_not(ahead))
    seam = jnp.logical_or(ahead, behind)
    in_turn = jnp.logical_and(has_crs, jnp.logical_not(seam))
    direct = jnp.logical_and(has_crs, turn)
    relayed = jnp.logical_and(has_crs, jnp.logical_not(turn))
    par = {"seq": s, "ch": o}
    sib = {"seq": sib_s, "ch": g}
    crs = {"seq": crs_s, "ch": g}
    dcr = {"seq": crs_s, "ch": o}
    dsb = {"seq": sib_s, "ch": o}
    cut = {"seq": cut_s, "ch": o}
    mates = [{"seq": x_next, "ch": g}, {"seq": x_last, "ch": g}, {"seq": s + z_step, "ch": g}]
    partners = [par, sib, dsb, cut] + mates

    barrier = pltpu.get_barrier_semaphore()
    for device in partners:
        pl.semaphore_signal(barrier, inc=1, device_id=device, device_id_type=MESH)

    @pl.when(has_crs)
    def _():
        for device in (crs, dcr):
            pl.semaphore_signal(barrier, inc=1, device_id=device, device_id_type=MESH)

    local = []

    def fetch(src, dst):
        copy = pltpu.make_async_copy(src, dst, local_sem.at[len(local)])
        copy.start()
        local.append(copy)
        return copy

    own_copy = fetch(stream, xr.at[g, 1])
    gain_copies = [
        fetch(norm_gain, ng), fetch(norm_shift, ns), fetch(mid_gain, mg), fetch(mid_shift, ms),
    ]
    cw0_copy = fetch(conv_weight.at[0], cw.at[0])
    mw0_copy = fetch(mix_weight.at[0], mw.at[0, g])
    cw1_copy = fetch(conv_weight.at[1], cw.at[1])
    mw1_copy = fetch(mix_weight.at[1], mw.at[1, g])
    up_copies = [fetch(up_gain, ug), fetch(up_shift, us), fetch(up_weight, uw), fetch(skip, skipb)]

    sends = []

    def send(src, dst, device, when=None, start=None):
        index = len(sends)
        copy = pltpu.make_async_remote_copy(
            src_ref=src, dst_ref=dst, send_sem=send_sem.at[index], recv_sem=recv_sem.at[index],
            device_id=device, device_id_type=MESH,
        )
        sends.append((copy, when))
        if when is None:
            copy.start()
        else:
            pl.when(when if start is None else start)(copy.start)
        return copy

    def arrive(*copies):
        for copy in copies:
            copy.wait_recv()

    def arrive_if(when, *copies):
        @pl.when(when)
        def _():
            for copy in copies:
                copy.wait_recv()

    def arrive_crs(*copies):
        arrive_if(has_crs, *copies)

    def weights(n, rows, device):
        return send(mw.at[n, o, rows], mw.at[n, o, rows], device)

    to_sib = 2 * core
    to_crs = 2 - 2 * core
    my_sib = 2 - 2 * core
    my_crs = 2 * core
    near = pl.ds(pl.multiple_of(32 * core, 32), 32)
    far = pl.ds(pl.multiple_of(32 - 32 * core, 32), 32)

    def piece(shift):
        quarter = lax.rem(x_at + 2 * z_bit + shift, 4)
        return pl.ds(pl.multiple_of(128 * core + 32 * quarter, 32), 32)

    pieces = [piece(0), piece(3), piece(1), piece(2)]

    own_copy.wait()
    @pl.when(jnp.logical_not(ahead))
    def _():
        pl.semaphore_wait(barrier, jnp.where(has_crs, len(partners) + 2, len(partners)))

    @pl.when(s == 0)
    def _():
        pl.semaphore_signal(go_sem, inc=1, device_id=cut, device_id_type=MESH)

    @pl.when(s == seq_devices // 2 + 1)
    def _():
        pl.semaphore_signal(go_sem, inc=1, device_id=sib, device_id_type=MESH)

    @pl.when(ahead)
    def _():
        pl.semaphore_wait(go_sem, 2)

    x_par = send(xr.at[g, 1, :, near], xr.at[g, 1, :, near], par)
    x_crs = send(xr.at[g, 1, :, near], xr.at[g, to_crs, :, near], crs, has_crs, at_once)
    x_dcr = send(xr.at[g, 1, :, near], xr.at[g, to_crs, :, near], dcr, direct, jnp.logical_and(direct, at_once))
    x_par2 = send(xr.at[g, 1, :, far], xr.at[g, 1, :, far], par)
    w_cut = [send(mix_weight.at[0, pieces[0]], mw.at[0, g, pieces[0]], cut)]
    x_sib = send(xr.at[g, 1], xr.at[g, to_sib], sib)
    x_crs2 = send(xr.at[g, 1, :, far], xr.at[g, to_crs, :, far], crs, has_crs, at_once)

    def activate0(gg, slot, rows, dst_row, valid):
        cols = pl.ds(pl.multiple_of(gg * 512, 512), 512)
        gain = ng[0:1, cols]
        shift = ns[0:1, cols]
        for b in range(2):
            v = gelu(xr[gg, slot, b, rows, :].astype(F32) * gain + shift)
            if valid is not None:
                v = jnp.where(valid, v, 0.0)
            a0[gg, b, dst_row, :] = v.astype(BF16)

    def conv0(gg):
        acc = None
        for k in range(3):
            term = dot(
                a0[gg, :, 32 * k : 32 * k + ROWS, :].reshape(128, 512),
                cw[0, k, pl.ds(pl.multiple_of(gg * 512, 512), 512), :],
            )
            acc = term if acc is None else acc + term
        return acc

    sib_src = pl.ds(pl.multiple_of(32 * core, 32), 32)
    crs_src = pl.ds(pl.multiple_of(32 - 32 * core, 32), 32)
    sib_dst = pl.ds(pl.multiple_of(96 - 96 * core, 32), 32)
    crs_dst = pl.ds(pl.multiple_of(96 * core, 32), 32)
    whole = pl.ds(0, ROWS)
    centre = pl.ds(32, ROWS)

    for copy in gain_copies:
        copy.wait()
    activate0(g, 1, whole, centre, None)
    arrive(x_sib)
    activate0(g, my_sib, sib_src, sib_dst, None)
    arrive_if(in_turn, x_crs)

    @pl.when(in_turn)
    def _():
        activate0(g, my_crs, crs_src, crs_dst, None)

    @pl.when(jnp.logical_not(in_turn))
    def _():
        a0[g, :, crs_dst, :] = jnp.zeros((2, 32, 512), BF16)


    @pl.when(ahead)
    def _():
        pl.semaphore_wait(barrier, len(partners) + 2)
        x_crs.start()
        x_dcr.start()
        x_crs2.start()

    arrive(x_par)
    x_near = send(xr.at[o, 1, :, near], xr.at[o, to_crs, :, near], crs, relayed)
    cw0_copy.wait()
    accf[...] = conv0(g)
    arrive(x_par2)
    x_fwd = send(xr.at[o, 1, :, far], xr.at[o, to_sib, :, far], sib)
    x_rel = send(xr.at[o, 1, :, far], xr.at[o, to_crs, :, far], crs, has_crs)
    activate0(o, 1, whole, centre, None)
    arrive(w_cut[0])
    w_mate = [[weights(0, pieces[0], mate) for mate in mates]]
    w_cut.append(send(mix_weight.at[1, pieces[0]], mw.at[1, g, pieces[0]], cut))
    w_fwd = [[weights(0, pieces[0], sib)]]
    x_fwd2 = send(xr.at[o, 1, :, near], xr.at[o, to_sib, :, near], sib)
    arrive(x_fwd)
    activate0(o, my_sib, sib_src, sib_dst, None)

    @pl.when(seam)
    def _():
        x_crs.wait_recv()
        activate0(g, my_crs, crs_src, crs_dst, None)
        accf[...] = conv0(g)

    arrive_if(direct, x_dcr)
    arrive_if(relayed, x_near)
    activate0(o, my_crs, crs_src, crs_dst, has_crs)
    acc = accf[...] + conv0(o)
    hb[g, 1] = gelu(acc * mg[0:1, :] + ms[0:1, :]).astype(BF16)

    h_own = hb.at[g, 1]
    h_par = send(h_own, hb.at[g, 1], par)
    h_dcr = send(h_own, hb.at[g, to_crs], dcr, direct)
    h_crs = send(h_own, hb.at[g, to_crs], crs, has_crs)
    h_sib = send(h_own, hb.at[g, to_sib], sib)


    def collect(n):
        for m in range(3):
            w_mate[n][m].wait_recv()
            w_fwd[n].append(weights(n, pieces[m + 1], sib))

    collect(0)

    def mix0(slot, valid):
        for n in range(4):
            cols = slice(256 * n, 256 * n + 256)
            gg, inner = n // 2, slice(256 * (n % 2), 256 * (n % 2) + 256)
            z = dot(hb[0, slot], mw[0, 0, :, cols]) + dot(hb[1, slot], mw[0, 1, :, cols])
            x = xr[gg, slot, :, :, inner].reshape(128, 256).astype(F32) + z
            x = x.astype(BF16)
            x1[slot, :, cols] = x
            v = gelu(x.astype(F32) * ng[1:2, cols] + ns[1:2, cols])
            if valid is not None:
                v = jnp.where(valid, v, 0.0)
            a1[slot, :, cols] = v.astype(BF16)
        return dot(a1[slot], cw[1, slot])

    mw0_copy.wait()
    cw1_copy.wait()
    arrive(h_par)
    h_fwd = send(hb.at[o, 1], hb.at[o, to_sib], sib)
    h_rel = send(hb.at[o, 1], hb.at[o, to_crs], crs, relayed)
    arrive(*w_fwd[0])
    acc = mix0(1, None)
    arrive(w_cut[1])
    w_mate.append([weights(1, pieces[0], mate) for mate in mates])
    w_fwd.append([weights(1, pieces[0], sib)])
    arrive(h_sib)
    arrive(h_fwd)
    arrive(x_fwd2)
    acc = acc + mix0(my_sib, None)
    arrive_crs(x_crs2)
    arrive_crs(x_rel)
    arrive_crs(h_crs)
    arrive_if(direct, h_dcr)
    arrive_if(relayed, h_rel)
    acc = acc + mix0(my_crs, has_crs)
    h1[g] = gelu(acc * mg[1:2, :] + ms[1:2, :]).astype(BF16).reshape(2, ROWS, 256)

    last = pl.ds(pl.multiple_of(48 - 48 * core, 16), 16)
    first = pl.ds(pl.multiple_of(48 * core, 16), 16)
    g_par = send(h1.at[g], h1.at[g], par)
    g_crs = send(h1.at[g, :, first], eh.at[g, 1 - core], crs, has_crs)
    g_dcr = send(h1.at[g, :, first], eh.at[g, 1 - core], dcr, has_crs)
    g_dsb = send(h1.at[g, :, last], eh.at[g, core], dsb)
    g_sib = send(h1.at[g, :, last], eh.at[g, core], sib)

    mw1_copy.wait()
    for copy in up_copies:
        copy.wait()

    edge_rows = [
        [slice(ROWS * b + 48 - 48 * side, ROWS * b + 64 - 48 * side) for b in range(2)] for side in range(2)
    ]

    def half_top(gg, first):
        for n in range(4):
            cols = slice(256 * n, 256 * n + 256)
            z = dot(h1[gg].reshape(128, 256), mw[1, gg, :, cols])
            if first:
                zf[:, cols] = z + x1[1, :, cols].astype(F32)
            else:
                v = (zf[:, cols] + z).astype(BF16).astype(F32)
                v = gelu(v * ug[0:1, cols] + us[0:1, cols]).astype(BF16).astype(F32)
                for b in range(2):
                    uf[b, 8 : 8 + ROWS, cols] = v[ROWS * b : ROWS * b + ROWS]

    def edge_top():
        for n in range(4):
            cols = slice(256 * n, 256 * n + 256)
            z = dot(eh[0].reshape(64, 256), mw[1, 0, :, cols]) + dot(eh[1].reshape(64, 256), mw[1, 1, :, cols])
            base = jnp.concatenate([x1[2 * side, rows, cols] for side in range(2) for rows in edge_rows[side]], axis=0)
            v = (base.astype(F32) + z).astype(BF16).astype(F32)
            v = gelu(v * ug[0:1, cols] + us[0:1, cols]).astype(BF16).astype(F32)
            for b in range(2):
                uf[b, 0:8, cols] = jnp.where(s > 0, v[16 * b + 8 : 16 * b + 16], 0.0)
                uf[b, 8 + ROWS : 16 + ROWS, cols] = jnp.where(
                    s < seq_devices - 1, v[32 + 16 * b : 32 + 16 * b + 8], 0.0
                )

    def rows_at(offset):
        return jnp.concatenate(
            [uf[b, 8 + offset : 8 + offset + ROWS, :].astype(BF16) for b in range(2)], axis=0
        )

    def centre_taps():
        here = rows_at(0)
        for r in range(4):
            cf[r] = dot(here, uw[2 + r])

    def outer_taps():
        for r in range(4):
            v = cf[r] + (dot(rows_at(-1), uw[6 + r]) if r < 2 else dot(rows_at(1), uw[r - 2]))
            for b in range(2):
                for half in range(2):
                    outf[b, half, pl.ds(r, ROWS, stride=4), :] = v[
                        ROWS * b : ROWS * b + ROWS, 128 * half : 128 * half + 128
                    ]

    def finish():
        for half in range(2):
            lanes = slice(128 * half, 128 * half + 128)
            out[:, :, lanes] = (outf[:, half] + skipb[:, :, lanes].astype(F32)).astype(BF16)

    collect(1)
    half_top(g, True)
    arrive(*w_fwd[1])
    arrive(g_par)
    half_top(o, False)
    centre_taps()
    arrive(g_sib, g_dsb)
    arrive_crs(g_crs, g_dcr)
    edge_top()
    outer_taps()
    finish()
    for copy, when in sends:
        if when is None:
            copy.wait_send()
        else:
            pl.when(when)(copy.wait_send)


def body(
    seq_devices, stream, skip, norm_gain, norm_shift, conv_weight, mid_gain, mid_shift, mix_weight, up_gain, up_shift, up_weight
):
    anywhere = pl.BlockSpec(memory_space=pl.ANY)
    return pl.pallas_call(
        functools.partial(kernel, seq_devices),
        name="bottleneck",
        out_shape=pltpu.VMEM((2, 256, 256), BF16),
        in_specs=[anywhere] * 11,
        out_specs=pl.BlockSpec(memory_space=pltpu.VMEM),
        scratch_shapes=[
            pltpu.VMEM((2, 3, 2, 64, 512), BF16),
            pltpu.VMEM((2, 2, 128, 512), BF16),
            pltpu.VMEM((2, 3, 128, 256), BF16),
            pltpu.VMEM((2, 2, 256, 1024), BF16),
            pltpu.VMEM((2, 3, 1024, 256), BF16),
            pltpu.VMEM((8, 1024, 256), BF16),
            pltpu.VMEM((3, 128, 1024), BF16),
            pltpu.VMEM((3, 128, 1024), BF16),
            pltpu.VMEM((2, 2, 64, 256), BF16),
            pltpu.VMEM((2, 2, 2, 16, 256), BF16),
            pltpu.VMEM((2, 80, 1024), F32),
            pltpu.VMEM((2, 2, 256, 128), F32),
            pltpu.VMEM((128, 1024), F32),
            pltpu.VMEM((4, 128, 256), F32),
            pltpu.VMEM((128, 256), F32),
            pltpu.VMEM((2, 256, 256), BF16),
            pltpu.VMEM((2, 1024), F32),
            pltpu.VMEM((2, 1024), F32),
            pltpu.VMEM((2, 256), F32),
            pltpu.VMEM((2, 256), F32),
            pltpu.VMEM((1, 1024), F32),
            pltpu.VMEM((1, 1024), F32),
            pltpu.SemaphoreType.DMA((16,)),
            pltpu.SemaphoreType.DMA((48,)),
            pltpu.SemaphoreType.DMA((48,)),
            pltpu.SemaphoreType.REGULAR,
        ],
        compiler_params=pltpu.CompilerParams(
            collective_id=0, has_side_effects=True, vmem_limit_bytes=56 * 1024 * 1024
        ),
    )(
        stream, skip, norm_gain, norm_shift, conv_weight, mid_gain, mid_shift, mix_weight,
        up_gain.reshape(1, -1), up_shift.reshape(1, -1), up_weight,
    )


def solution(mesh):
    placed = (
        P(None, "seq", "ch"),
        P(None, "seq", "ch"),
        P(),
        P(),
        P(None, None, None, "ch"),
        P(None, "ch"),
        P(None, "ch"),
        P(None, "ch", None),
        P(),
        P(),
        P(None, None, "ch"),
    )
    return jax.shard_map(
        functools.partial(body, mesh.shape["seq"]),
        mesh=mesh, in_specs=placed, out_specs=P(None, "seq", "ch"), check_vma=False,
    )
```

```python
import functools

import jax
import jax.numpy as jnp
from jax import lax
from jax.experimental import pallas as pl
from jax.experimental.pallas import tpu as pltpu
from jax.sharding import PartitionSpec as P

MESH = pl.DeviceIdType.MESH
F32 = jnp.float32
BF16 = jnp.bfloat16
ROWS = 64
LOCALS = 13
LANDINGS = 21
GELU_A = 0.7978845608028654
GELU_B = 0.7978845608028654 * 0.044715


def gelu(v):
    half = 0.5 * v
    return half + half * jnp.tanh(v * (GELU_A + GELU_B * (v * v)))


def dot(a, b):
    return jnp.dot(a, b, preferred_element_type=F32)


def kernel(
    seq_devices,
    stream, skip, norm_gain, norm_shift, conv_weight, mid_gain, mid_shift, mix_weight, up_gain, up_shift, up_weight,
    out,
    xr, a0, hb, mw, cw, uw, a1, x1, h1, eh, uf, outf, zf, cf, accf, skipb, ng, ns, mg, ms, ug, us,
    local_sem, send_sem, recv_sem, go_sem,
):
    s = lax.axis_index("seq")
    g = lax.axis_index("ch")
    core = lax.rem(s, 2)
    o = 1 - g
    sib_s = s + 1 - 2 * core
    crs_s = lax.rem(s + seq_devices - 1 + 2 * core, seq_devices)
    cut_s = lax.rem(s + seq_devices // 2, seq_devices)
    x_at = lax.rem(s // 2, 4)
    z_bit = lax.rem(s // 8, 2)
    row = s - 2 * x_at
    x_next = row + 2 * lax.rem(x_at + 1, 4)
    x_last = row + 2 * lax.rem(x_at + 3, 4)
    z_step = 8 - 16 * z_bit
    y_bit = s // (seq_devices // 2)
    has_crs = jnp.logical_and(s > 0, s < seq_devices - 1)
    ahead = s == seq_devices // 2
    behind = s == seq_devices // 2 - 1
    turn = lax.rem(s, 8) == 7 * core
    at_once = jnp.logical_and(has_crs, jnp.logical_not(ahead))
    seam = jnp.logical_or(ahead, behind)
    in_turn = jnp.logical_and(has_crs, jnp.logical_not(seam))
    direct = jnp.logical_and(has_crs, turn)
    relayed = jnp.logical_and(has_crs, jnp.logical_not(turn))
    par = {"seq": s, "ch": o}
    sib = {"seq": sib_s, "ch": g}
    crs = {"seq": crs_s, "ch": g}
    dcr = {"seq": crs_s, "ch": o}
    dsb = {"seq": sib_s, "ch": o}
    cut = {"seq": cut_s, "ch": o}
    mates = [{"seq": x_next, "ch": g}, {"seq": x_last, "ch": g}, {"seq": s + z_step, "ch": g}]
    partners = [par, sib, dsb, cut] + mates

    barrier = pltpu.get_barrier_semaphore()
    for device in partners:
        pl.semaphore_signal(barrier, inc=1, device_id=device, device_id_type=MESH)

    @pl.when(has_crs)
    def _():
        for device in (crs, dcr):
            pl.semaphore_signal(barrier, inc=1, device_id=device, device_id_type=MESH)

    local = []

    def fetch(src, dst):
        copy = pltpu.make_async_copy(src, dst, local_sem.at[len(local)])
        copy.start()
        local.append(copy)
        return copy

    own_copy = fetch(stream, xr.at[g, 1])
    gain_copies = [
        fetch(norm_gain, ng), fetch(norm_shift, ns), fetch(mid_gain, mg), fetch(mid_shift, ms),
    ]
    cw0_copy = fetch(conv_weight.at[0], cw.at[0])
    mw0_copy = fetch(mix_weight.at[0], mw.at[0, g])
    cw1_copy = fetch(conv_weight.at[1], cw.at[1])
    mw1_copy = fetch(mix_weight.at[1], mw.at[1, g])
    up_copies = [fetch(up_gain, ug), fetch(up_shift, us), fetch(up_weight, uw), fetch(skip, skipb)]

    sends = []
    names = {}

    def landing(name):
        return recv_sem.at[names.setdefault(name, len(names))]

    def send(name, src, dst, device, when=None, start=None):
        copy = pltpu.make_async_remote_copy(
            src_ref=src, dst_ref=dst, send_sem=send_sem.at[0], recv_sem=landing(name),
            device_id=device, device_id_type=MESH,
        )
        sends.append((copy, when))
        if when is None:
            copy.start()
        else:
            pl.when(when if start is None else start)(copy.start)
        return copy

    def arrive(name, block):
        pltpu.make_async_remote_copy(
            src_ref=block, dst_ref=block, send_sem=send_sem.at[0], recv_sem=landing(name),
            device_id=par, device_id_type=MESH,
        ).wait_recv()

    def arrive_if(when, name, block):
        pl.when(when)(functools.partial(arrive, name, block))

    def weights(name, n, rows, device):
        return send(name, mw.at[n, o, rows], mw.at[n, o, rows], device)

    def drain():
        for copy, when in sends:
            if when is None:
                copy.wait_send()
        for group in (has_crs, direct, relayed):
            some = [copy for copy, when in sends if when is group]

            @pl.when(group)
            def _():
                for copy in some:
                    copy.wait_send()

    to_sib = 2 * core
    to_crs = 2 - 2 * core
    my_sib = 2 - 2 * core
    my_crs = 2 * core
    near = pl.ds(pl.multiple_of(32 * core, 32), 32)
    far = pl.ds(pl.multiple_of(32 - 32 * core, 32), 32)

    def piece(shift):
        quarter = lax.rem(x_at + 2 * z_bit + shift, 4)
        return pl.ds(pl.multiple_of(128 * core + 32 * quarter, 32), 32)

    mine = pl.ds(pl.multiple_of(128 * core, 128), 128)
    theirs = pl.ds(pl.multiple_of(128 - 128 * core, 128), 128)
    pieces = [piece(0), piece(3), piece(1), piece(2)]

    own_copy.wait()
    @pl.when(jnp.logical_not(ahead))
    def _():
        pl.semaphore_wait(barrier, jnp.where(has_crs, len(partners) + 2, len(partners)))

    @pl.when(s == 0)
    def _():
        pl.semaphore_signal(go_sem, inc=1, device_id=cut, device_id_type=MESH)

    @pl.when(s == seq_devices // 2 + 1)
    def _():
        pl.semaphore_signal(go_sem, inc=1, device_id=sib, device_id_type=MESH)

    @pl.when(ahead)
    def _():
        pl.semaphore_wait(go_sem, 2)

    for b in range(2):
        send(f"x_par{b}", xr.at[g, 1, b, near], xr.at[g, 1, b, near], par)
    x_crs = send("x_crs", xr.at[g, 1, :, near], xr.at[g, to_crs, :, near], crs, has_crs, at_once)
    x_dcr = send("x_near", xr.at[g, 1, :, near], xr.at[g, to_crs, :, near], dcr, direct, jnp.logical_and(direct, at_once))
    send("x_par2", xr.at[g, 1, :, far], xr.at[g, 1, :, far], par)
    send("w_cut0", mix_weight.at[0, pieces[0]], mw.at[0, g, pieces[0]], cut)
    send("x_sib", xr.at[g, 1], xr.at[g, to_sib], sib)
    x_crs2 = send("x_far", xr.at[g, 1, :, far], xr.at[g, to_crs, :, far], crs, has_crs, at_once)

    def activate0(gg, slot, rows, dst_row, valid):
        cols = pl.ds(pl.multiple_of(gg * 512, 512), 512)
        gain = ng[0:1, cols]
        shift = ns[0:1, cols]
        for b in range(2):
            v = gelu(xr[gg, slot, b, rows, :].astype(F32) * gain + shift)
            if valid is not None:
                v = jnp.where(valid, v, 0.0)
            a0[gg, b, dst_row, :] = v.astype(BF16)

    def conv0(gg):
        acc = None
        for k in range(3):
            term = dot(
                a0[gg, :, 32 * k : 32 * k + ROWS, :].reshape(128, 512),
                cw[0, k, pl.ds(pl.multiple_of(gg * 512, 512), 512), :],
            )
            acc = term if acc is None else acc + term
        return acc

    sib_src = pl.ds(pl.multiple_of(32 * core, 32), 32)
    crs_src = pl.ds(pl.multiple_of(32 - 32 * core, 32), 32)
    sib_dst = pl.ds(pl.multiple_of(96 - 96 * core, 32), 32)
    crs_dst = pl.ds(pl.multiple_of(96 * core, 32), 32)
    whole = pl.ds(0, ROWS)
    centre = pl.ds(32, ROWS)

    for copy in gain_copies:
        copy.wait()
    activate0(g, 1, whole, centre, None)
    arrive("x_sib", xr.at[g, my_sib])
    activate0(g, my_sib, sib_src, sib_dst, None)
    arrive_if(in_turn, "x_crs", xr.at[g, my_crs, :, far])

    @pl.when(in_turn)
    def _():
        activate0(g, my_crs, crs_src, crs_dst, None)

    @pl.when(jnp.logical_not(in_turn))
    def _():
        a0[g, :, crs_dst, :] = jnp.zeros((2, 32, 512), BF16)

    @pl.when(ahead)
    def _():
        pl.semaphore_wait(barrier, len(partners) + 2)
        x_crs.start()
        x_dcr.start()
        x_crs2.start()

    for b in range(2):
        arrive(f"x_par{b}", xr.at[o, 1, b, near])
        send("x_near", xr.at[o, 1, b, near], xr.at[o, to_crs, b, near], crs, relayed)
    cw0_copy.wait()
    accf[...] = conv0(g)
    arrive("x_par2", xr.at[o, 1, :, far])
    send("x_fwd", xr.at[o, 1, :, far], xr.at[o, to_sib, :, far], sib)
    send("x_far", xr.at[o, 1, :, far], xr.at[o, to_crs, :, far], crs, has_crs)
    activate0(o, 1, whole, centre, None)
    arrive("w_cut0", mw.at[0, o, pieces[0]])
    for m in range(3):
        weights(f"w_mate{m}", 0, pieces[0], mates[m])
    send("w_cut1", mix_weight.at[1, pieces[0]], mw.at[1, g, pieces[0]], cut)
    weights("w_fwd0", 0, pieces[0], sib)
    send("x_fwd2", xr.at[o, 1, :, near], xr.at[o, to_sib, :, near], sib)
    arrive("x_fwd", xr.at[o, my_sib, :, near])
    activate0(o, my_sib, sib_src, sib_dst, None)

    @pl.when(seam)
    def _():
        arrive("x_crs", xr.at[g, my_crs, :, far])
        activate0(g, my_crs, crs_src, crs_dst, None)
        accf[...] = conv0(g)

    arrive_if(has_crs, "x_near", xr.at[o, my_crs, :, far])
    activate0(o, my_crs, crs_src, crs_dst, has_crs)
    acc = accf[...] + conv0(o)
    hb[g, 1] = gelu(acc * mg[0:1, :] + ms[0:1, :]).astype(BF16)

    halves = [pl.ds(ROWS * b, ROWS) for b in range(2)]
    for b in range(2):
        send(f"h_par{b}", hb.at[g, 1, halves[b]], hb.at[g, 1, halves[b]], par)
    send("h_crs", hb.at[g, 1], hb.at[g, to_crs], dcr, direct)
    send("h_crs", hb.at[g, 1], hb.at[g, to_crs], crs, has_crs)
    send("h_sib", hb.at[g, 1], hb.at[g, to_sib], sib)
    for m in range(3):
        arrive(f"w_mate{m}", mw.at[0, o, pieces[m + 1]])
        weights("w_fwd0", 0, pieces[m + 1], sib)

    def mix0(slot, valid):
        for n in range(4):
            cols = slice(256 * n, 256 * n + 256)
            gg, inner = n // 2, slice(256 * (n % 2), 256 * (n % 2) + 256)
            z = dot(hb[0, slot], mw[0, 0, :, cols]) + dot(hb[1, slot], mw[0, 1, :, cols])
            x = xr[gg, slot, :, :, inner].reshape(128, 256).astype(F32) + z
            x = x.astype(BF16)
            x1[slot, :, cols] = x
            v = gelu(x.astype(F32) * ng[1:2, cols] + ns[1:2, cols])
            if valid is not None:
                v = jnp.where(valid, v, 0.0)
            a1[slot, :, cols] = v.astype(BF16)
        return dot(a1[slot], cw[1, slot])

    mw0_copy.wait()
    cw1_copy.wait()
    for b in range(2):
        arrive(f"h_par{b}", hb.at[o, 1, halves[b]])
        send("h_crs", hb.at[o, 1, halves[b]], hb.at[o, to_crs, halves[b]], crs, relayed)
        send("h_sib", hb.at[o, 1, halves[b]], hb.at[o, to_sib, halves[b]], sib)
    arrive("w_fwd0", mw.at[0, o, theirs])
    acc = mix0(1, None)
    arrive("w_cut1", mw.at[1, o, pieces[0]])
    for mate in mates:
        weights("w_mate", 1, pieces[0], mate)
    arrive("h_sib", hb.at[:, my_sib])
    arrive("x_fwd2", xr.at[o, my_sib, :, far])
    acc = acc + mix0(my_sib, None)
    arrive_if(has_crs, "x_far", xr.at[:, my_crs, :, near])
    arrive_if(has_crs, "h_crs", hb.at[:, my_crs])
    acc = acc + mix0(my_crs, has_crs)
    h1[g] = gelu(acc * mg[1:2, :] + ms[1:2, :]).astype(BF16).reshape(2, ROWS, 256)

    last = pl.ds(pl.multiple_of(48 - 48 * core, 16), 16)
    first = pl.ds(pl.multiple_of(48 * core, 16), 16)
    send("x_par0", h1.at[g], h1.at[g], par)
    send("x_crs", h1.at[g, :, first], eh.at[g, 1 - core], crs, has_crs)
    send("x_crs", h1.at[g, :, first], eh.at[g, 1 - core], dcr, has_crs)
    send("x_sib", h1.at[g, :, last], eh.at[g, core], dsb)
    send("x_sib", h1.at[g, :, last], eh.at[g, core], sib)

    mw1_copy.wait()
    for copy in up_copies:
        copy.wait()

    edge_rows = [
        [slice(ROWS * b + 48 - 48 * side, ROWS * b + 64 - 48 * side) for b in range(2)] for side in range(2)
    ]

    def half_top(gg, first):
        for n in range(4):
            cols = slice(256 * n, 256 * n + 256)
            z = dot(h1[gg].reshape(128, 256), mw[1, gg, :, cols])
            if first:
                zf[:, cols] = z + x1[1, :, cols].astype(F32)
            else:
                v = (zf[:, cols] + z).astype(BF16).astype(F32)
                v = gelu(v * ug[0:1, cols] + us[0:1, cols]).astype(BF16).astype(F32)
                for b in range(2):
                    uf[b, 8 : 8 + ROWS, cols] = v[ROWS * b : ROWS * b + ROWS]

    def edge_top():
        for n in range(4):
            cols = slice(256 * n, 256 * n + 256)
            z = dot(eh[0].reshape(64, 256), mw[1, 0, :, cols]) + dot(eh[1].reshape(64, 256), mw[1, 1, :, cols])
            base = jnp.concatenate([x1[2 * side, rows, cols] for side in range(2) for rows in edge_rows[side]], axis=0)
            v = (base.astype(F32) + z).astype(BF16).astype(F32)
            v = gelu(v * ug[0:1, cols] + us[0:1, cols]).astype(BF16).astype(F32)
            for b in range(2):
                uf[b, 0:8, cols] = jnp.where(s > 0, v[16 * b + 8 : 16 * b + 16], 0.0)
                uf[b, 8 + ROWS : 16 + ROWS, cols] = jnp.where(
                    s < seq_devices - 1, v[32 + 16 * b : 32 + 16 * b + 8], 0.0
                )

    def rows_at(offset):
        return jnp.concatenate(
            [uf[b, 8 + offset : 8 + offset + ROWS, :].astype(BF16) for b in range(2)], axis=0
        )

    def centre_taps():
        here = rows_at(0)
        for r in range(4):
            cf[r] = dot(here, uw[2 + r])

    def outer_taps():
        for r in range(4):
            v = cf[r] + (dot(rows_at(-1), uw[6 + r]) if r < 2 else dot(rows_at(1), uw[r - 2]))
            for b in range(2):
                for half in range(2):
                    outf[b, half, pl.ds(r, ROWS, stride=4), :] = v[
                        ROWS * b : ROWS * b + ROWS, 128 * half : 128 * half + 128
                    ]

    def finish():
        for half in range(2):
            lanes = slice(128 * half, 128 * half + 128)
            out[:, :, lanes] = (outf[:, half] + skipb[:, :, lanes].astype(F32)).astype(BF16)

    arrive("w_mate", mw.at[1, o, pl.ds(0, 96)])
    weights("w_fwd1", 1, mine, sib)
    half_top(g, True)
    arrive("w_fwd1", mw.at[1, o, theirs])
    arrive("x_par0", h1.at[o])
    half_top(o, False)
    centre_taps()
    arrive("x_sib", eh.at[:, 1 - core])
    arrive_if(has_crs, "x_crs", eh.at[:, core])
    edge_top()
    outer_taps()
    finish()
    drain()
    assert len(names) == LANDINGS and len(local) == LOCALS


def body(
    seq_devices, stream, skip, norm_gain, norm_shift, conv_weight, mid_gain, mid_shift, mix_weight, up_gain, up_shift, up_weight
):
    anywhere = pl.BlockSpec(memory_space=pl.ANY)
    return pl.pallas_call(
        functools.partial(kernel, seq_devices),
        name="bottleneck",
        out_shape=pltpu.VMEM((2, 256, 256), BF16),
        in_specs=[anywhere] * 11,
        out_specs=pl.BlockSpec(memory_space=pltpu.VMEM),
        scratch_shapes=[
            pltpu.VMEM((2, 3, 2, 64, 512), BF16),
            pltpu.VMEM((2, 2, 128, 512), BF16),
            pltpu.VMEM((2, 3, 128, 256), BF16),
            pltpu.VMEM((2, 2, 256, 1024), BF16),
            pltpu.VMEM((2, 3, 1024, 256), BF16),
            pltpu.VMEM((8, 1024, 256), BF16),
            pltpu.VMEM((3, 128, 1024), BF16),
            pltpu.VMEM((3, 128, 1024), BF16),
            pltpu.VMEM((2, 2, 64, 256), BF16),
            pltpu.VMEM((2, 2, 2, 16, 256), BF16),
            pltpu.VMEM((2, 80, 1024), F32),
            pltpu.VMEM((2, 2, 256, 128), F32),
            pltpu.VMEM((128, 1024), F32),
            pltpu.VMEM((4, 128, 256), F32),
            pltpu.VMEM((128, 256), F32),
            pltpu.VMEM((2, 256, 256), BF16),
            pltpu.VMEM((2, 1024), F32),
            pltpu.VMEM((2, 1024), F32),
            pltpu.VMEM((2, 256), F32),
            pltpu.VMEM((2, 256), F32),
            pltpu.VMEM((1, 1024), F32),
            pltpu.VMEM((1, 1024), F32),
            pltpu.SemaphoreType.DMA((LOCALS,)),
            pltpu.SemaphoreType.DMA((1,)),
            pltpu.SemaphoreType.DMA((LANDINGS,)),
            pltpu.SemaphoreType.REGULAR,
        ],
        compiler_params=pltpu.CompilerParams(
            collective_id=0, has_side_effects=True, vmem_limit_bytes=56 * 1024 * 1024
        ),
    )(
        stream, skip, norm_gain, norm_shift, conv_weight, mid_gain, mid_shift, mix_weight,
        up_gain.reshape(1, -1), up_shift.reshape(1, -1), up_weight,
    )


def solution(mesh):
    placed = (
        P(None, "seq", "ch"),
        P(None, "seq", "ch"),
        P(),
        P(),
        P(None, None, None, "ch"),
        P(None, "ch"),
        P(None, "ch"),
        P(None, "ch", None),
        P(),
        P(),
        P(None, None, "ch"),
    )
    return jax.shard_map(
        functools.partial(body, mesh.shape["seq"]),
        mesh=mesh, in_specs=placed, out_specs=P(None, "seq", "ch"), check_vma=False,
    )
```

```python
import functools

import jax
import jax.numpy as jnp
from jax import lax
from jax.experimental import pallas as pl
from jax.experimental.pallas import tpu as pltpu
from jax.sharding import PartitionSpec as P

MESH = pl.DeviceIdType.MESH
F32 = jnp.float32
BF16 = jnp.bfloat16
ROWS = 64
LOCALS = 13
LANDINGS = 26
GELU_A = 0.7978845608028654
GELU_B = 0.7978845608028654 * 0.044715


def gelu(v):
    half = 0.5 * v
    return half + half * jnp.tanh(v * (GELU_A + GELU_B * (v * v)))


def dot(a, b):
    return jnp.dot(a, b, preferred_element_type=F32)


def kernel(
    seq_devices,
    stream, skip, norm_gain, norm_shift, conv_weight, mid_gain, mid_shift, mix_weight, up_gain, up_shift, up_weight,
    out,
    xr, a0, hb, mw, cw, uw, a1, x1, h1, eh, ex, eg, ea, uf, outf, zf, cf, accf, skipb, ng, ns, mg, ms, ug, us,
    local_sem, send_sem, recv_sem, go_sem, known_sem,
):
    s = lax.axis_index("seq")
    g = lax.axis_index("ch")
    core = lax.rem(s, 2)
    o = 1 - g
    sib_s = s + 1 - 2 * core
    crs_s = lax.rem(s + seq_devices - 1 + 2 * core, seq_devices)
    cut_s = lax.rem(s + seq_devices // 2, seq_devices)
    x_at = lax.rem(s // 2, 4)
    z_bit = lax.rem(s // 8, 2)
    row = s - 2 * x_at
    x_next = row + 2 * lax.rem(x_at + 1, 4)
    x_last = row + 2 * lax.rem(x_at + 3, 4)
    z_step = 8 - 16 * z_bit
    y_bit = s // (seq_devices // 2)
    has_crs = jnp.logical_and(s > 0, s < seq_devices - 1)
    ahead = s == seq_devices // 2
    behind = s == seq_devices // 2 - 1
    turn = lax.rem(s, 8) == 7 * core
    at_once = jnp.logical_and(has_crs, jnp.logical_not(ahead))
    seam = jnp.logical_or(ahead, behind)
    feeder = s == seq_devices // 2 - 2
    crs_edges = jnp.logical_and(has_crs, jnp.logical_not(behind))
    in_turn = jnp.logical_and(has_crs, jnp.logical_not(seam))
    direct = jnp.logical_and(has_crs, turn)
    direct_edges = jnp.logical_and(direct, jnp.logical_not(behind))
    relayed = jnp.logical_and(has_crs, jnp.logical_not(turn))
    par = {"seq": s, "ch": o}
    sib = {"seq": sib_s, "ch": g}
    crs = {"seq": crs_s, "ch": g}
    dcr = {"seq": crs_s, "ch": o}
    dsb = {"seq": sib_s, "ch": o}
    cut = {"seq": cut_s, "ch": o}
    mates = [{"seq": x_next, "ch": g}, {"seq": x_last, "ch": g}, {"seq": s + z_step, "ch": g}]
    partners = [par, sib, cut] + mates
    middle = s // 2 == seq_devices // 4

    barrier = pltpu.get_barrier_semaphore()
    for device in partners:
        pl.semaphore_signal(barrier, inc=1, device_id=device, device_id_type=MESH)

    back = [{"seq": lax.rem(s + seq_devices - 2, seq_devices), "ch": ch} for ch in (g, o)]
    fed = [{"seq": lax.rem(s + 2, seq_devices), "ch": ch} for ch in (g, o)]
    for device, when in ((crs, has_crs), (dcr, direct), (dsb, middle), (back[0], ahead), (back[1], ahead)):
        pl.when(when)(functools.partial(
            pl.semaphore_signal, barrier, inc=1, device_id=device, device_id_type=MESH
        ))

    local = []

    def fetch(src, dst):
        copy = pltpu.make_async_copy(src, dst, local_sem.at[len(local)])
        copy.start()
        local.append(copy)
        return copy

    own_copy = fetch(stream, xr.at[g, 1])
    gain_copies = [
        fetch(norm_gain, ng), fetch(norm_shift, ns), fetch(mid_gain, mg), fetch(mid_shift, ms),
    ]
    cw0_copy = fetch(conv_weight.at[0], cw.at[0])
    mw0_copy = fetch(mix_weight.at[0], mw.at[0, g])
    cw1_copy = fetch(conv_weight.at[1], cw.at[1])
    mw1_copy = fetch(mix_weight.at[1], mw.at[1, g])
    up_copies = [fetch(up_gain, ug), fetch(up_shift, us), fetch(up_weight, uw), fetch(skip, skipb)]

    sends = []
    names = {}

    def landing(name):
        return recv_sem.at[names.setdefault(name, len(names))]

    def send(name, src, dst, device, when=None, start=None):
        copy = pltpu.make_async_remote_copy(
            src_ref=src, dst_ref=dst, send_sem=send_sem.at[0], recv_sem=landing(name),
            device_id=device, device_id_type=MESH,
        )
        sends.append((copy, when))
        if when is None:
            copy.start()
        else:
            pl.when(when if start is None else start)(copy.start)
        return copy

    def arrive(name, block):
        pltpu.make_async_remote_copy(
            src_ref=block, dst_ref=block, send_sem=send_sem.at[0], recv_sem=landing(name),
            device_id=par, device_id_type=MESH,
        ).wait_recv()

    def arrive_if(when, name, block):
        pl.when(when)(functools.partial(arrive, name, block))

    def weights(name, n, rows, device):
        return send(name, mw.at[n, o, rows], mw.at[n, o, rows], device)

    def drain():
        for copy, when in sends:
            if when is None:
                copy.wait_send()
        for group in (has_crs, direct, relayed, ahead, crs_edges, direct_edges, feeder):
            some = [copy for copy, when in sends if when is group]

            @pl.when(group)
            def _():
                for copy in some:
                    copy.wait_send()

    to_sib = 2 * core
    to_crs = 2 - 2 * core
    my_sib = 2 - 2 * core
    my_crs = 2 * core
    near = pl.ds(pl.multiple_of(32 * core, 32), 32)
    far = pl.ds(pl.multiple_of(32 - 32 * core, 32), 32)

    def piece(shift):
        quarter = lax.rem(x_at + 2 * z_bit + shift, 4)
        return pl.ds(pl.multiple_of(128 * core + 32 * quarter, 32), 32)

    theirs = pl.ds(pl.multiple_of(128 - 128 * core, 128), 128)
    pieces = [piece(0), piece(3), piece(1), piece(2)]

    own_copy.wait()
    entered = len(partners) + has_crs.astype(jnp.int32) + direct.astype(jnp.int32) + middle.astype(jnp.int32)
    entered = entered + 2 * feeder.astype(jnp.int32)

    @pl.when(jnp.logical_not(ahead))
    def _():
        pl.semaphore_wait(barrier, entered)

    @pl.when(s == 0)
    def _():
        pl.semaphore_signal(go_sem, inc=1, device_id=cut, device_id_type=MESH)

    @pl.when(s == seq_devices // 2 + 1)
    def _():
        pl.semaphore_signal(go_sem, inc=1, device_id=sib, device_id_type=MESH)

    @pl.when(ahead)
    def _():
        pl.semaphore_wait(go_sem, 2)

    def vouch():
        pl.semaphore_signal(known_sem, inc=1, device_id=sib, device_id_type=MESH)
        pl.when(has_crs)(functools.partial(
            pl.semaphore_signal, known_sem, inc=1, device_id=crs, device_id_type=MESH
        ))

    pl.when(jnp.logical_not(ahead))(vouch)

    for b in range(2):
        send(f"x_par{b}", xr.at[g, 1, b, near], xr.at[g, 1, b, near], par)
    x_crs = send("x_crs", xr.at[g, 1, :, near], xr.at[g, to_crs, :, near], crs, has_crs, at_once)
    x_dcr = send("x_near", xr.at[g, 1, :, near], xr.at[g, to_crs, :, near], dcr, direct, jnp.logical_and(direct, at_once))
    send("x_par2", xr.at[g, 1, :, far], xr.at[g, 1, :, far], par)
    send("w_cut0", mix_weight.at[0, pieces[0]], mw.at[0, g, pieces[0]], cut)
    send("x_sib", xr.at[g, 1], xr.at[g, to_sib], sib)
    x_crs2 = send("x_far", xr.at[g, 1, :, far], xr.at[g, to_crs, :, far], crs, has_crs, at_once)
    for device in fed:
        send("x_feed", xr.at[g, 1, :, pl.ds(48, 16)], ex.at[g], device, feeder)

    def activate0(gg, slot, rows, dst_row, valid):
        cols = pl.ds(pl.multiple_of(gg * 512, 512), 512)
        gain = ng[0:1, cols]
        shift = ns[0:1, cols]
        for b in range(2):
            v = gelu(xr[gg, slot, b, rows, :].astype(F32) * gain + shift)
            if valid is not None:
                v = jnp.where(valid, v, 0.0)
            a0[gg, b, dst_row, :] = v.astype(BF16)

    def conv0(gg):
        acc = None
        for k in range(3):
            term = dot(
                a0[gg, :, 32 * k : 32 * k + ROWS, :].reshape(128, 512),
                cw[0, k, pl.ds(pl.multiple_of(gg * 512, 512), 512), :],
            )
            acc = term if acc is None else acc + term
        return acc

    sib_src = pl.ds(pl.multiple_of(32 * core, 32), 32)
    crs_src = pl.ds(pl.multiple_of(32 - 32 * core, 32), 32)
    sib_dst = pl.ds(pl.multiple_of(96 - 96 * core, 32), 32)
    crs_dst = pl.ds(pl.multiple_of(96 * core, 32), 32)
    whole = pl.ds(0, ROWS)
    centre = pl.ds(32, ROWS)

    for copy in gain_copies:
        copy.wait()
    activate0(g, 1, whole, centre, None)
    arrive("x_sib", xr.at[g, my_sib])
    activate0(g, my_sib, sib_src, sib_dst, None)
    arrive_if(in_turn, "x_crs", xr.at[g, my_crs, :, far])

    @pl.when(in_turn)
    def _():
        activate0(g, my_crs, crs_src, crs_dst, None)

    @pl.when(jnp.logical_not(in_turn))
    def _():
        a0[g, :, crs_dst, :] = jnp.zeros((2, 32, 512), BF16)

    @pl.when(ahead)
    def _():
        pl.semaphore_wait(barrier, entered)
        x_crs.start()
        x_dcr.start()

    for b in range(2):
        arrive(f"x_par{b}", xr.at[o, 1, b, near])
        send("x_near", xr.at[o, 1, b, near], xr.at[o, to_crs, b, near], crs, relayed)
    cw0_copy.wait()
    accf[...] = conv0(g)
    arrive("x_par2", xr.at[o, 1, :, far])
    send("x_fwd", xr.at[o, 1, :, far], xr.at[o, to_sib, :, far], sib)
    send("x_far", xr.at[o, 1, :, far], xr.at[o, to_crs, :, far], crs, has_crs)
    send("w_cut1", mix_weight.at[1, pieces[0]], mw.at[1, g, pieces[0]], cut)
    activate0(o, 1, whole, centre, None)
    arrive("w_cut0", mw.at[0, o, pieces[0]])
    for m in range(3):
        weights(f"w_mate{m}", 0, pieces[0], mates[m])
    weights("w_fwd0", 0, pieces[0], sib)
    send("x_fwd2", xr.at[o, 1, :, near], xr.at[o, to_sib, :, near], sib)
    arrive("x_fwd", xr.at[o, my_sib, :, near])
    activate0(o, my_sib, sib_src, sib_dst, None)

    pl.when(ahead)(x_crs2.start)
    pl.when(ahead)(vouch)

    @pl.when(seam)
    def _():
        arrive("x_crs", xr.at[g, my_crs, :, far])
        activate0(g, my_crs, crs_src, crs_dst, None)
        accf[...] = conv0(g)

    arrive_if(has_crs, "x_near", xr.at[o, my_crs, :, far])
    activate0(o, my_crs, crs_src, crs_dst, has_crs)
    acc = accf[...] + conv0(o)
    hb[g, 1] = gelu(acc * mg[0:1, :] + ms[0:1, :]).astype(BF16)

    halves = [pl.ds(ROWS * b, ROWS) for b in range(2)]
    for b in range(2):
        send(f"h_crs{b}", hb.at[g, 1, halves[b]], hb.at[g, to_crs, halves[b]], dcr, direct)
    for b in range(2):
        send(f"h_par{b}", hb.at[g, 1, halves[b]], hb.at[g, 1, halves[b]], par)
    for b in range(2):
        send(f"h_crs{b}", hb.at[g, 1, halves[b]], hb.at[g, to_crs, halves[b]], crs, has_crs)
    send("h_sib", hb.at[g, 1], hb.at[g, to_sib], sib)
    for device in fed:
        for b in range(2):
            send("h_feed", hb.at[g, 1, pl.ds(ROWS * b + 48, 16)], eg.at[g, pl.ds(16 * b, 16)], device, feeder)
    for m in range(3):
        arrive(f"w_mate{m}", mw.at[0, o, pieces[m + 1]])
        weights("w_fwd0", 0, pieces[m + 1], sib)

    def mix0(slot, valid, rows, batch):
        count = rows.stop - rows.start
        for n in range(4):
            cols = slice(256 * n, 256 * n + 256)
            gg, inner = n // 2, slice(256 * (n % 2), 256 * (n % 2) + 256)
            z = dot(hb[0, slot, rows], mw[0, 0, :, cols]) + dot(hb[1, slot, rows], mw[0, 1, :, cols])
            x = xr[gg, slot, batch, :, inner].reshape(count, 256).astype(F32) + z
            x = x.astype(BF16)
            x1[slot, rows, cols] = x
            v = gelu(x.astype(F32) * ng[1:2, cols] + ns[1:2, cols])
            if valid is not None:
                v = jnp.where(valid, v, 0.0)
            a1[slot, rows, cols] = v.astype(BF16)
        return dot(a1[slot, rows], cw[1, slot])

    last = pl.ds(pl.multiple_of(48 - 48 * core, 16), 16)
    first = pl.ds(pl.multiple_of(48 * core, 16), 16)
    every = slice(0, 128)
    both = slice(0, 2)
    mw0_copy.wait()
    cw1_copy.wait()
    for b in range(2):
        arrive(f"h_par{b}", hb.at[o, 1, halves[b]])
        send(f"h_crs{b}", hb.at[o, 1, halves[b]], hb.at[o, to_crs, halves[b]], crs, relayed)
        send("h_sib", hb.at[o, 1, halves[b]], hb.at[o, to_sib, halves[b]], sib)
    arrive("w_cut1", mw.at[1, o, pieces[0]])
    for m in range(3):
        weights(f"w_mate{m + 3}", 1, pieces[0], mates[m])
    weights("w_fwd1", 1, pieces[0], sib)
    arrive("w_fwd0", mw.at[0, o, theirs])
    acc = mix0(1, None, every, both)
    arrive("h_sib", hb.at[:, my_sib])
    arrive("x_fwd2", xr.at[o, my_sib, :, far])
    acc = acc + mix0(my_sib, None, every, both)
    arrive_if(has_crs, "x_far", xr.at[:, my_crs, :, near])
    for b in range(2):
        rows = slice(ROWS * b, ROWS * b + ROWS)
        arrive_if(has_crs, f"h_crs{b}", hb.at[:, my_crs, rows])
        part = acc[rows] + mix0(my_crs, has_crs, rows, slice(b, b + 1))
        h1[g, b] = gelu(part * mg[1:2, :] + ms[1:2, :]).astype(BF16)
        if b == 1:
            send("x_crs", h1.at[g, :, first], eh.at[g, 1 - core], dcr, direct_edges)
        send(f"x_par{b}", h1.at[g, b], h1.at[g, b], par)

    pl.semaphore_wait(known_sem, 1 + has_crs.astype(jnp.int32))
    send("x_crs", h1.at[g, :, first], eh.at[g, 1 - core], crs, crs_edges)
    send("x_crs", h1.at[g, :, first], eh.at[g, 1 - core], dcr, relayed)
    send("x_sib", h1.at[g, :, last], eh.at[g, core], dsb)
    send("x_sib", h1.at[g, :, last], eh.at[g, core], sib)

    def edge_behind():
        arrive("x_feed", ex)
        arrive("h_feed", eg)
        for n in range(4):
            cols = slice(256 * n, 256 * n + 256)
            gg, inner = n // 2, slice(256 * (n % 2), 256 * (n % 2) + 256)
            z = dot(eg[0], mw[0, 0, :, cols]) + dot(eg[1], mw[0, 1, :, cols])
            x = (ex[gg, :, :, inner].reshape(32, 256).astype(F32) + z).astype(BF16).astype(F32)
            ea[:, cols] = gelu(x * ng[1:2, cols] + ns[1:2, cols]).astype(BF16)
        y = dot(ea[...], cw[1, 0])
        for k in range(2):
            tail = jnp.concatenate([a1[k, ROWS * b + 48 : ROWS * b + ROWS, :] for b in range(2)], axis=0)
            y = y + dot(tail, cw[1, k + 1])
        eh[g, 0] = gelu(y * mg[1:2, :] + ms[1:2, :]).astype(BF16).reshape(2, 16, 256)

    pl.when(ahead)(edge_behind)
    send("x_crs", eh.at[g, 0], eh.at[g, 0], par, ahead)

    mw1_copy.wait()
    for copy in up_copies:
        copy.wait()

    edge_rows = [
        [slice(ROWS * b + 48 - 48 * side, ROWS * b + 64 - 48 * side) for b in range(2)] for side in range(2)
    ]

    def half_top():
        for n in range(4):
            cols = slice(256 * n, 256 * n + 256)
            zf[:, cols] = dot(h1[g].reshape(128, 256), mw[1, g, :, cols]) + x1[1, :, cols].astype(F32)

    def whole_top(b):
        rows = slice(ROWS * b, ROWS * b + ROWS)
        for n in range(4):
            cols = slice(256 * n, 256 * n + 256)
            v = (zf[rows, cols] + dot(h1[o, b], mw[1, o, :, cols])).astype(BF16).astype(F32)
            v = gelu(v * ug[0:1, cols] + us[0:1, cols])
            uf[b, 8 : 8 + ROWS, cols] = v.astype(BF16).astype(F32)

    def edge_top():
        for n in range(4):
            cols = slice(256 * n, 256 * n + 256)
            z = dot(eh[0].reshape(64, 256), mw[1, 0, :, cols]) + dot(eh[1].reshape(64, 256), mw[1, 1, :, cols])
            base = jnp.concatenate([x1[2 * side, rows, cols] for side in range(2) for rows in edge_rows[side]], axis=0)
            v = (base.astype(F32) + z).astype(BF16).astype(F32)
            v = gelu(v * ug[0:1, cols] + us[0:1, cols]).astype(BF16).astype(F32)
            for b in range(2):
                uf[b, 0:8, cols] = jnp.where(s > 0, v[16 * b + 8 : 16 * b + 16], 0.0)
                uf[b, 8 + ROWS : 16 + ROWS, cols] = jnp.where(
                    s < seq_devices - 1, v[32 + 16 * b : 32 + 16 * b + 8], 0.0
                )

    def rows_at(offset):
        return jnp.concatenate(
            [uf[b, 8 + offset : 8 + offset + ROWS, :].astype(BF16) for b in range(2)], axis=0
        )

    def centre_taps():
        here = rows_at(0)
        for r in range(4):
            cf[r] = dot(here, uw[2 + r])

    def outer_taps():
        for r in range(4):
            v = cf[r] + (dot(rows_at(-1), uw[6 + r]) if r < 2 else dot(rows_at(1), uw[r - 2]))
            for b in range(2):
                for half in range(2):
                    outf[b, half, pl.ds(r, ROWS, stride=4), :] = v[
                        ROWS * b : ROWS * b + ROWS, 128 * half : 128 * half + 128
                    ]

    def finish():
        for half in range(2):
            lanes = slice(128 * half, 128 * half + 128)
            out[:, :, lanes] = (outf[:, half] + skipb[:, :, lanes].astype(F32)).astype(BF16)

    for m in range(3):
        arrive(f"w_mate{m + 3}", mw.at[1, o, pieces[m + 1]])
        weights("w_fwd1", 1, pieces[m + 1], sib)
    half_top()
    arrive("w_fwd1", mw.at[1, o, theirs])
    for b in range(2):
        arrive(f"x_par{b}", h1.at[o, b])
        whole_top(b)
    centre_taps()
    arrive("x_sib", eh.at[:, 1 - core])
    arrive_if(at_once, "x_crs", eh.at[:, core])
    arrive_if(ahead, "x_crs", eh.at[o, core])
    edge_top()
    outer_taps()
    finish()
    drain()
    assert len(names) == LANDINGS and len(local) == LOCALS


def body(
    seq_devices, stream, skip, norm_gain, norm_shift, conv_weight, mid_gain, mid_shift, mix_weight, up_gain, up_shift, up_weight
):
    anywhere = pl.BlockSpec(memory_space=pl.ANY)
    return pl.pallas_call(
        functools.partial(kernel, seq_devices),
        name="bottleneck",
        out_shape=pltpu.VMEM((2, 256, 256), BF16),
        in_specs=[anywhere] * 11,
        out_specs=pl.BlockSpec(memory_space=pltpu.VMEM),
        scratch_shapes=[
            pltpu.VMEM((2, 3, 2, 64, 512), BF16),
            pltpu.VMEM((2, 2, 128, 512), BF16),
            pltpu.VMEM((2, 3, 128, 256), BF16),
            pltpu.VMEM((2, 2, 256, 1024), BF16),
            pltpu.VMEM((2, 3, 1024, 256), BF16),
            pltpu.VMEM((8, 1024, 256), BF16),
            pltpu.VMEM((3, 128, 1024), BF16),
            pltpu.VMEM((3, 128, 1024), BF16),
            pltpu.VMEM((2, 2, 64, 256), BF16),
            pltpu.VMEM((2, 2, 2, 16, 256), BF16),
            pltpu.VMEM((2, 2, 16, 512), BF16),
            pltpu.VMEM((2, 32, 256), BF16),
            pltpu.VMEM((32, 1024), BF16),
            pltpu.VMEM((2, 80, 1024), F32),
            pltpu.VMEM((2, 2, 256, 128), F32),
            pltpu.VMEM((128, 1024), F32),
            pltpu.VMEM((4, 128, 256), F32),
            pltpu.VMEM((128, 256), F32),
            pltpu.VMEM((2, 256, 256), BF16),
            pltpu.VMEM((2, 1024), F32),
            pltpu.VMEM((2, 1024), F32),
            pltpu.VMEM((2, 256), F32),
            pltpu.VMEM((2, 256), F32),
            pltpu.VMEM((1, 1024), F32),
            pltpu.VMEM((1, 1024), F32),
            pltpu.SemaphoreType.DMA((LOCALS,)),
            pltpu.SemaphoreType.DMA((1,)),
            pltpu.SemaphoreType.DMA((LANDINGS,)),
            pltpu.SemaphoreType.REGULAR,
            pltpu.SemaphoreType.REGULAR,
        ],
        compiler_params=pltpu.CompilerParams(
            collective_id=0, has_side_effects=True, vmem_limit_bytes=56 * 1024 * 1024
        ),
    )(
        stream, skip, norm_gain, norm_shift, conv_weight, mid_gain, mid_shift, mix_weight,
        up_gain.reshape(1, -1), up_shift.reshape(1, -1), up_weight,
    )


def solution(mesh):
    placed = (
        P(None, "seq", "ch"),
        P(None, "seq", "ch"),
        P(),
        P(),
        P(None, None, None, "ch"),
        P(None, "ch"),
        P(None, "ch"),
        P(None, "ch", None),
        P(),
        P(),
        P(None, None, "ch"),
    )
    return jax.shard_map(
        functools.partial(body, mesh.shape["seq"]),
        mesh=mesh, in_specs=placed, out_specs=P(None, "seq", "ch"), check_vma=False,
    )
```

```python
import functools

import jax
import jax.numpy as jnp
from jax import lax
from jax.experimental import pallas as pl
from jax.experimental.pallas import tpu as pltpu
from jax.sharding import PartitionSpec as P

MESH = pl.DeviceIdType.MESH
F32 = jnp.float32
BF16 = jnp.bfloat16
ROWS = 64
LOCALS = 10
LANDINGS = 26
GELU_A = 0.7978845608028654
GELU_B = 0.7978845608028654 * 0.044715


def gelu(v):
    half = 0.5 * v
    return half + half * jnp.tanh(v * (GELU_A + GELU_B * (v * v)))


def dot(a, b):
    return jnp.dot(a, b, preferred_element_type=F32)


def kernel(
    seq_devices,
    stream, skip, norm_gain, norm_shift, conv_weight, mid_gain, mid_shift, mix_weight, up_gain, up_shift, up_weight,
    out,
    xr, a0, hb, mw, cw, uw, a1, x1, h1, eh, ex, eg, ea, uf, outf, zf, cf, accf, skipb, norms, mids, ups,
    local_sem, send_sem, recv_sem, go_sem, known_sem,
):
    s = lax.axis_index("seq")
    g = lax.axis_index("ch")
    core = lax.rem(s, 2)
    o = 1 - g
    sib_s = s + 1 - 2 * core
    crs_s = lax.rem(s + seq_devices - 1 + 2 * core, seq_devices)
    cut_s = lax.rem(s + seq_devices // 2, seq_devices)
    z_bit = lax.rem(s // 8, 2)
    z_step = 8 - 16 * z_bit
    y_bit = s // (seq_devices // 2)
    has_crs = jnp.logical_and(s > 0, s < seq_devices - 1)
    ahead = s == seq_devices // 2
    behind = s == seq_devices // 2 - 1
    turn = lax.rem(s, 8) == 7 * core
    at_once = jnp.logical_and(has_crs, jnp.logical_not(ahead))
    seam = jnp.logical_or(ahead, behind)
    feeder = s == seq_devices // 2 - 2
    crs_edges = jnp.logical_and(has_crs, jnp.logical_not(behind))
    in_turn = jnp.logical_and(has_crs, jnp.logical_not(seam))
    direct = jnp.logical_and(has_crs, turn)
    direct_edges = jnp.logical_and(direct, jnp.logical_not(behind))
    relayed = jnp.logical_and(has_crs, jnp.logical_not(turn))
    par = {"seq": s, "ch": o}
    sib = {"seq": sib_s, "ch": g}
    crs = {"seq": crs_s, "ch": g}
    dcr = {"seq": crs_s, "ch": o}
    dsb = {"seq": sib_s, "ch": o}
    cut = {"seq": cut_s, "ch": o}
    x_bit = lax.rem(s // 2, 2)
    x_pair = s + 2 - 4 * x_bit
    mates = [{"seq": x_pair + z_step, "ch": g}, {"seq": x_pair, "ch": g}, {"seq": s + z_step, "ch": g}]
    partners = [par, sib, cut] + mates
    middle = s // 2 == seq_devices // 4

    barrier = pltpu.get_barrier_semaphore()
    for device in partners:
        pl.semaphore_signal(barrier, inc=1, device_id=device, device_id_type=MESH)

    back = [{"seq": lax.rem(s + seq_devices - 2, seq_devices), "ch": ch} for ch in (g, o)]
    fed = [{"seq": lax.rem(s + 2, seq_devices), "ch": ch} for ch in (g, o)]
    for device, when in ((crs, has_crs), (dcr, direct), (dsb, middle), (back[0], ahead), (back[1], ahead)):
        pl.when(when)(functools.partial(
            pl.semaphore_signal, barrier, inc=1, device_id=device, device_id_type=MESH
        ))

    local = []

    def fetch(src, dst):
        copy = pltpu.make_async_copy(src, dst, local_sem.at[len(local)])
        copy.start()
        local.append(copy)
        return copy

    def fetch_pair(first_src, second_src, dst):
        both_here = pltpu.make_async_copy(dst, dst, local_sem.at[len(local)])
        for k, src in enumerate((first_src, second_src)):
            pltpu.make_async_copy(src, dst.at[k], local_sem.at[len(local)]).start()
        local.append(both_here)

    own_copy = fetch(stream, xr.at[g, 1])
    fetch_pair(norm_gain, norm_shift, norms)
    fetch_pair(mid_gain, mid_shift, mids)
    cw0_copy = fetch(conv_weight.at[0], cw.at[0])
    mw0_copy = fetch(mix_weight.at[0], mw.at[0, g])
    cw1_copy = fetch(conv_weight.at[1], cw.at[1])
    mw1_copy = fetch(mix_weight.at[1], mw.at[1, g])
    up_copies = [fetch(up_weight, uw), fetch(skip, skipb)]
    fetch_pair(up_gain, up_shift, ups)
    ng, ns, mg, ms, ug, us = norms.at[0], norms.at[1], mids.at[0], mids.at[1], ups.at[0], ups.at[1]

    sends = []
    names = {}

    def landing(name):
        return recv_sem.at[names.setdefault(name, len(names))]

    def send(name, src, dst, device, when=None, start=None):
        copy = pltpu.make_async_remote_copy(
            src_ref=src, dst_ref=dst, send_sem=send_sem.at[0], recv_sem=landing(name),
            device_id=device, device_id_type=MESH,
        )
        sends.append((copy, when))
        if when is None:
            copy.start()
        else:
            pl.when(when if start is None else start)(copy.start)
        return copy

    def arrive(name, block):
        pltpu.make_async_remote_copy(
            src_ref=block, dst_ref=block, send_sem=send_sem.at[0], recv_sem=landing(name),
            device_id=par, device_id_type=MESH,
        ).wait_recv()

    def arrive_if(when, name, block):
        pl.when(when)(functools.partial(arrive, name, block))

    def weights(name, n, rows, device):
        return send(name, mw.at[n, o, rows], mw.at[n, o, rows], device)

    def drain():
        for copy, when in sends:
            if when is None:
                copy.wait_send()
        for group in (has_crs, direct, relayed, ahead, crs_edges, direct_edges, feeder):
            some = [copy for copy, when in sends if when is group]

            @pl.when(group)
            def _():
                for copy in some:
                    copy.wait_send()

    to_sib = my_sib = 0
    to_crs = my_crs = 2
    sib_side = 2 - 2 * core
    crs_side = 2 * core
    near = pl.ds(pl.multiple_of(32 * core, 32), 32)
    far = pl.ds(pl.multiple_of(32 - 32 * core, 32), 32)

    def piece(x, z):
        return pl.ds(pl.multiple_of(128 * core + 32 * x + 64 * z, 32), 32)

    theirs = pl.ds(pl.multiple_of(128 - 128 * core, 128), 128)
    pieces = [piece(x_bit, z_bit), piece(1 - x_bit, 1 - z_bit), piece(1 - x_bit, z_bit), piece(x_bit, 1 - z_bit)]

    own_copy.wait()
    entered = len(partners) + has_crs.astype(jnp.int32) + direct.astype(jnp.int32) + middle.astype(jnp.int32)
    entered = entered + 2 * feeder.astype(jnp.int32)

    @pl.when(jnp.logical_not(ahead))
    def _():
        pl.semaphore_wait(barrier, entered)

    @pl.when(s == 0)
    def _():
        pl.semaphore_signal(go_sem, inc=1, device_id=cut, device_id_type=MESH)

    @pl.when(s == seq_devices // 2 + 1)
    def _():
        pl.semaphore_signal(go_sem, inc=1, device_id=sib, device_id_type=MESH)

    @pl.when(ahead)
    def _():
        pl.semaphore_wait(go_sem, 2)

    def vouch():
        pl.semaphore_signal(known_sem, inc=1, device_id=sib, device_id_type=MESH)
        pl.when(has_crs)(functools.partial(
            pl.semaphore_signal, known_sem, inc=1, device_id=crs, device_id_type=MESH
        ))

    pl.when(jnp.logical_not(ahead))(vouch)

    for b in range(2):
        send(f"x_par{b}", xr.at[g, 1, b, near], xr.at[g, 1, b, near], par)
    x_crs = send("x_crs", xr.at[g, 1, :, near], xr.at[g, to_crs, :, near], crs, has_crs, at_once)
    x_dcr = send("x_near", xr.at[g, 1, :, near], xr.at[g, to_crs, :, near], dcr, direct, jnp.logical_and(direct, at_once))
    send("w_cut0", mix_weight.at[0, pieces[0]], mw.at[0, g, pieces[0]], cut)
    send("x_par2", xr.at[g, 1, :, far], xr.at[g, 1, :, far], par)
    send("x_sib", xr.at[g, 1], xr.at[g, to_sib], sib)
    x_crs2 = send("x_far", xr.at[g, 1, :, far], xr.at[g, to_crs, :, far], crs, has_crs, at_once)
    for device in fed:
        send("x_feed", xr.at[g, 1, :, pl.ds(48, 16)], ex.at[g], device, feeder)

    def activate0(gg, slot, rows, dst_row, valid):
        cols = pl.ds(pl.multiple_of(gg * 512, 512), 512)
        gain = ng[0:1, cols]
        shift = ns[0:1, cols]
        for b in range(2):
            v = gelu(xr[gg, slot, b, rows, :].astype(F32) * gain + shift)
            if valid is not None:
                v = jnp.where(valid, v, 0.0)
            a0[gg, b, dst_row, :] = v.astype(BF16)

    def conv0(gg):
        acc = None
        for k in range(3):
            term = dot(
                a0[gg, :, 32 * k : 32 * k + ROWS, :].reshape(128, 512),
                cw[0, k, pl.ds(pl.multiple_of(gg * 512, 512), 512), :],
            )
            acc = term if acc is None else acc + term
        return acc

    sib_src = pl.ds(pl.multiple_of(32 * core, 32), 32)
    crs_src = pl.ds(pl.multiple_of(32 - 32 * core, 32), 32)
    sib_dst = pl.ds(pl.multiple_of(96 - 96 * core, 32), 32)
    crs_dst = pl.ds(pl.multiple_of(96 * core, 32), 32)
    whole = pl.ds(0, ROWS)
    centre = pl.ds(32, ROWS)

    for copy in local[1:3]:
        copy.wait()
    activate0(g, 1, whole, centre, None)
    arrive("x_sib", xr.at[g, my_sib])
    activate0(g, my_sib, sib_src, sib_dst, None)
    arrive_if(in_turn, "x_crs", xr.at[g, my_crs, :, far])

    @pl.when(in_turn)
    def _():
        activate0(g, my_crs, crs_src, crs_dst, None)

    @pl.when(jnp.logical_not(in_turn))
    def _():
        a0[g, :, crs_dst, :] = jnp.zeros((2, 32, 512), BF16)

    @pl.when(ahead)
    def _():
        pl.semaphore_wait(barrier, entered)
        x_crs.start()
        x_dcr.start()

    for b in range(2):
        arrive(f"x_par{b}", xr.at[o, 1, b, near])
        send("x_near", xr.at[o, 1, b, near], xr.at[o, to_crs, b, near], crs, relayed)
    cw0_copy.wait()
    accf[...] = conv0(g)
    arrive("x_par2", xr.at[o, 1, :, far])
    send("x_fwd", xr.at[o, 1, :, far], xr.at[o, to_sib, :, far], sib)
    send("x_far", xr.at[o, 1, :, far], xr.at[o, to_crs, :, far], crs, has_crs)
    send("w_cut1", mix_weight.at[1, pieces[0]], mw.at[1, g, pieces[0]], cut)
    activate0(o, 1, whole, centre, None)
    arrive("w_cut0", mw.at[0, o, pieces[0]])
    for m in range(3):
        weights(f"w_mate{m}", 0, pieces[0], mates[m])
    weights("w_fwd0", 0, pieces[0], sib)
    send("x_fwd2", xr.at[o, 1, :, near], xr.at[o, to_sib, :, near], sib)
    arrive("x_fwd", xr.at[o, my_sib, :, near])
    activate0(o, my_sib, sib_src, sib_dst, None)

    pl.when(ahead)(x_crs2.start)
    pl.when(ahead)(vouch)

    @pl.when(seam)
    def _():
        arrive("x_crs", xr.at[g, my_crs, :, far])
        activate0(g, my_crs, crs_src, crs_dst, None)
        accf[...] = conv0(g)

    arrive_if(has_crs, "x_near", xr.at[o, my_crs, :, far])
    activate0(o, my_crs, crs_src, crs_dst, has_crs)
    acc = accf[...] + conv0(o)
    hb[g, 1] = gelu(acc * mg[0:1, :] + ms[0:1, :]).astype(BF16)

    halves = [pl.ds(ROWS * b, ROWS) for b in range(2)]
    for b in range(2):
        send(f"h_crs{b}", hb.at[g, 1, halves[b]], hb.at[g, to_crs, halves[b]], dcr, direct)
    for b in range(2):
        send(f"h_par{b}", hb.at[g, 1, halves[b]], hb.at[g, 1, halves[b]], par)
    for b in range(2):
        send(f"h_crs{b}", hb.at[g, 1, halves[b]], hb.at[g, to_crs, halves[b]], crs, has_crs)
    send("h_sib", hb.at[g, 1], hb.at[g, to_sib], sib)
    for device in fed:
        for b in range(2):
            send("h_feed", hb.at[g, 1, pl.ds(ROWS * b + 48, 16)], eg.at[g, pl.ds(16 * b, 16)], device, feeder)
    for m in range(3):
        arrive(f"w_mate{m}", mw.at[0, o, pieces[m + 1]])
        weights("w_fwd0", 0, pieces[m + 1], sib)

    def mix0(slot, tap, valid, rows, batch):
        count = rows.stop - rows.start
        for n in range(4):
            cols = slice(256 * n, 256 * n + 256)
            gg, inner = n // 2, slice(256 * (n % 2), 256 * (n % 2) + 256)
            z = dot(hb[0, slot, rows], mw[0, 0, :, cols]) + dot(hb[1, slot, rows], mw[0, 1, :, cols])
            x = xr[gg, slot, batch, :, inner].reshape(count, 256).astype(F32) + z
            x = x.astype(BF16)
            x1[slot, rows, cols] = x
            v = gelu(x.astype(F32) * ng[1:2, cols] + ns[1:2, cols])
            if valid is not None:
                v = jnp.where(valid, v, 0.0)
            a1[slot, rows, cols] = v.astype(BF16)
        return dot(a1[slot, rows], cw[1, tap])

    last = pl.ds(pl.multiple_of(48 - 48 * core, 16), 16)
    first = pl.ds(pl.multiple_of(48 * core, 16), 16)
    every = slice(0, 128)
    both = slice(0, 2)
    mw0_copy.wait()
    cw1_copy.wait()
    for b in range(2):
        arrive(f"h_par{b}", hb.at[o, 1, halves[b]])
        send(f"h_crs{b}", hb.at[o, 1, halves[b]], hb.at[o, to_crs, halves[b]], crs, relayed)
        send("h_sib", hb.at[o, 1, halves[b]], hb.at[o, to_sib, halves[b]], sib)
    arrive("w_cut1", mw.at[1, o, pieces[0]])
    for m in range(3):
        weights(f"w_mate{m + 3}", 1, pieces[0], mates[m])
    weights("w_fwd1", 1, pieces[0], sib)
    arrive("w_fwd0", mw.at[0, o, theirs])
    acc = mix0(1, 1, None, every, both)
    arrive("h_sib", hb.at[:, my_sib])
    arrive("x_fwd2", xr.at[o, my_sib, :, far])
    acc = acc + mix0(my_sib, sib_side, None, every, both)
    arrive_if(has_crs, "x_far", xr.at[:, my_crs, :, near])
    for b in range(2):
        rows = slice(ROWS * b, ROWS * b + ROWS)
        arrive_if(has_crs, f"h_crs{b}", hb.at[:, my_crs, rows])
        part = acc[rows] + mix0(my_crs, crs_side, has_crs, rows, slice(b, b + 1))
        h1[g, b] = gelu(part * mg[1:2, :] + ms[1:2, :]).astype(BF16)
        if b == 1:
            send("x_crs", h1.at[g, :, first], eh.at[g, 1 - core], dcr, direct_edges)
        send(f"x_par{b}", h1.at[g, b], h1.at[g, b], par)

    pl.semaphore_wait(known_sem, 1 + has_crs.astype(jnp.int32))
    send("x_crs", h1.at[g, :, first], eh.at[g, 1 - core], crs, crs_edges)
    send("x_crs", h1.at[g, :, first], eh.at[g, 1 - core], dcr, relayed)
    send("x_sib", h1.at[g, :, last], eh.at[g, core], dsb)
    send("x_sib", h1.at[g, :, last], eh.at[g, core], sib)

    def edge_behind():
        arrive("x_feed", ex)
        arrive("h_feed", eg)
        for n in range(4):
            cols = slice(256 * n, 256 * n + 256)
            gg, inner = n // 2, slice(256 * (n % 2), 256 * (n % 2) + 256)
            z = dot(eg[0], mw[0, 0, :, cols]) + dot(eg[1], mw[0, 1, :, cols])
            x = (ex[gg, :, :, inner].reshape(32, 256).astype(F32) + z).astype(BF16).astype(F32)
            ea[:, cols] = gelu(x * ng[1:2, cols] + ns[1:2, cols]).astype(BF16)
        y = dot(ea[...], cw[1, 0])
        for k in range(2):
            tail = jnp.concatenate([a1[2 - k, ROWS * b + 48 : ROWS * b + ROWS, :] for b in range(2)], axis=0)
            y = y + dot(tail, cw[1, k + 1])
        eh[g, 0] = gelu(y * mg[1:2, :] + ms[1:2, :]).astype(BF16).reshape(2, 16, 256)

    pl.when(ahead)(edge_behind)
    send("x_crs", eh.at[g, 0], eh.at[g, 0], par, ahead)

    mw1_copy.wait()
    for copy in up_copies + local[-1:]:
        copy.wait()

    def half_top():
        for n in range(4):
            cols = slice(256 * n, 256 * n + 256)
            zf[:, cols] = dot(h1[g].reshape(128, 256), mw[1, g, :, cols]) + x1[1, :, cols].astype(F32)

    def whole_top(b):
        rows = slice(ROWS * b, ROWS * b + ROWS)
        for n in range(4):
            cols = slice(256 * n, 256 * n + 256)
            v = (zf[rows, cols] + dot(h1[o, b], mw[1, o, :, cols])).astype(BF16).astype(F32)
            v = gelu(v * ug[0:1, cols] + us[0:1, cols])
            uf[b, 8 : 8 + ROWS, cols] = v.astype(BF16).astype(F32)

    def edge_top():
        left, right = 2 - 2 * core, 2 * core
        for n in range(4):
            cols = slice(256 * n, 256 * n + 256)
            z = dot(eh[0].reshape(64, 256), mw[1, 0, :, cols]) + dot(eh[1].reshape(64, 256), mw[1, 1, :, cols])
            for b in range(2):
                for base, part, valid, to in (
                    (x1[left, ROWS * b + 48 : ROWS * b + ROWS, cols].astype(F32)[8:], z[16 * b + 8 : 16 * b + 16],
                     s > 0, slice(0, 8)),
                    (x1[right, ROWS * b : ROWS * b + 16, cols].astype(F32)[:8], z[32 + 16 * b : 40 + 16 * b],
                     s < seq_devices - 1, slice(8 + ROWS, 16 + ROWS)),
                ):
                    v = (base + part).astype(BF16).astype(F32)
                    v = gelu(v * ug[0:1, cols] + us[0:1, cols]).astype(BF16).astype(F32)
                    uf[b, to, cols] = jnp.where(valid, v, 0.0)

    def rows_at(offset):
        return jnp.concatenate(
            [uf[b, 8 + offset : 8 + offset + ROWS, :].astype(BF16) for b in range(2)], axis=0
        )

    def centre_taps():
        here = rows_at(0)
        for r in range(4):
            cf[r] = dot(here, uw[2 + r])

    def outer_taps():
        for r in range(4):
            v = cf[r] + (dot(rows_at(-1), uw[6 + r]) if r < 2 else dot(rows_at(1), uw[r - 2]))
            for b in range(2):
                for half in range(2):
                    outf[b, half, pl.ds(r, ROWS, stride=4), :] = v[
                        ROWS * b : ROWS * b + ROWS, 128 * half : 128 * half + 128
                    ]

    def finish():
        for half in range(2):
            lanes = slice(128 * half, 128 * half + 128)
            out[:, :, lanes] = (outf[:, half] + skipb[:, :, lanes].astype(F32)).astype(BF16)

    for m in range(3):
        arrive(f"w_mate{m + 3}", mw.at[1, o, pieces[m + 1]])
        weights("w_fwd1", 1, pieces[m + 1], sib)
    half_top()
    arrive("w_fwd1", mw.at[1, o, theirs])
    for b in range(2):
        arrive(f"x_par{b}", h1.at[o, b])
        whole_top(b)
    centre_taps()
    arrive("x_sib", eh.at[:, 1 - core])
    arrive_if(at_once, "x_crs", eh.at[:, core])
    arrive_if(ahead, "x_crs", eh.at[o, core])
    edge_top()
    outer_taps()
    finish()
    drain()
    assert len(names) == LANDINGS and len(local) == LOCALS


def body(
    seq_devices, stream, skip, norm_gain, norm_shift, conv_weight, mid_gain, mid_shift, mix_weight, up_gain, up_shift, up_weight
):
    anywhere = pl.BlockSpec(memory_space=pl.ANY)
    return pl.pallas_call(
        functools.partial(kernel, seq_devices),
        name="bottleneck",
        out_shape=pltpu.VMEM((2, 256, 256), BF16),
        in_specs=[anywhere] * 11,
        out_specs=pl.BlockSpec(memory_space=pltpu.VMEM),
        scratch_shapes=[
            pltpu.VMEM((2, 3, 2, 64, 512), BF16),
            pltpu.VMEM((2, 2, 128, 512), BF16),
            pltpu.VMEM((2, 3, 128, 256), BF16),
            pltpu.VMEM((2, 2, 256, 1024), BF16),
            pltpu.VMEM((2, 3, 1024, 256), BF16),
            pltpu.VMEM((8, 1024, 256), BF16),
            pltpu.VMEM((3, 128, 1024), BF16),
            pltpu.VMEM((3, 128, 1024), BF16),
            pltpu.VMEM((2, 2, 64, 256), BF16),
            pltpu.VMEM((2, 2, 2, 16, 256), BF16),
            pltpu.VMEM((2, 2, 16, 512), BF16),
            pltpu.VMEM((2, 32, 256), BF16),
            pltpu.VMEM((32, 1024), BF16),
            pltpu.VMEM((2, 80, 1024), F32),
            pltpu.VMEM((2, 2, 256, 128), F32),
            pltpu.VMEM((128, 1024), F32),
            pltpu.VMEM((4, 128, 256), F32),
            pltpu.VMEM((128, 256), F32),
            pltpu.VMEM((2, 256, 256), BF16),
            pltpu.VMEM((2, 2, 1024), F32),
            pltpu.VMEM((2, 2, 256), F32),
            pltpu.VMEM((2, 1, 1024), F32),
            pltpu.SemaphoreType.DMA((LOCALS,)),
            pltpu.SemaphoreType.DMA((1,)),
            pltpu.SemaphoreType.DMA((LANDINGS,)),
            pltpu.SemaphoreType.REGULAR,
            pltpu.SemaphoreType.REGULAR,
        ],
        compiler_params=pltpu.CompilerParams(
            collective_id=0, has_side_effects=True, vmem_limit_bytes=56 * 1024 * 1024
        ),
    )(
        stream, skip, norm_gain, norm_shift, conv_weight, mid_gain, mid_shift, mix_weight,
        up_gain.reshape(1, -1), up_shift.reshape(1, -1), up_weight,
    )


def solution(mesh):
    placed = (
        P(None, "seq", "ch"),
        P(None, "seq", "ch"),
        P(),
        P(),
        P(None, None, None, "ch"),
        P(None, "ch"),
        P(None, "ch"),
        P(None, "ch", None),
        P(),
        P(),
        P(None, None, "ch"),
    )
    return jax.shard_map(
        functools.partial(body, mesh.shape["seq"]),
        mesh=mesh, in_specs=placed, out_specs=P(None, "seq", "ch"), check_vma=False,
    )
```

```python
import functools

import jax
import jax.numpy as jnp
from jax import lax
from jax.experimental import pallas as pl
from jax.experimental.pallas import tpu as pltpu
from jax.sharding import PartitionSpec as P

MESH = pl.DeviceIdType.MESH
F32 = jnp.float32
BF16 = jnp.bfloat16
ROWS = 64
LOCALS = 10
LANDINGS = 26
GELU_A = 0.7978845608028654
GELU_B = 0.7978845608028654 * 0.044715


def gelu(v):
    half = 0.5 * v
    return half + half * jnp.tanh(v * (GELU_A + GELU_B * (v * v)))


def dot(a, b):
    return jnp.dot(a, b, preferred_element_type=F32)


def kernel(
    seq_devices,
    stream, skip, norm_gain, norm_shift, conv_weight, mid_gain, mid_shift, mix_weight, up_gain, up_shift, up_weight,
    out,
    xr, a0, hb, mw, cw, uw, a1, x1, h1, eh, ex, eg, ea, uf, outf, zf, cf, accf, skipb, norms, mids, ups,
    local_sem, send_sem, recv_sem, go_sem, known_sem,
):
    s = lax.axis_index("seq")
    g = lax.axis_index("ch")
    core = lax.rem(s, 2)
    o = 1 - g
    sib_s = s + 1 - 2 * core
    crs_s = lax.rem(s + seq_devices - 1 + 2 * core, seq_devices)
    cut_s = lax.rem(s + seq_devices // 2, seq_devices)
    z_bit = lax.rem(s // 8, 2)
    z_step = 8 - 16 * z_bit
    y_bit = s // (seq_devices // 2)
    has_crs = jnp.logical_and(s > 0, s < seq_devices - 1)
    ahead = s == seq_devices // 2
    behind = s == seq_devices // 2 - 1
    turn = lax.rem(s, 8) == 7 * core
    at_once = jnp.logical_and(has_crs, jnp.logical_not(ahead))
    seam = jnp.logical_or(ahead, behind)
    feeder = s == seq_devices // 2 - 2
    crs_edges = jnp.logical_and(has_crs, jnp.logical_not(behind))
    in_turn = jnp.logical_and(has_crs, jnp.logical_not(seam))
    direct = jnp.logical_and(has_crs, turn)
    direct_edges = jnp.logical_and(direct, jnp.logical_not(behind))
    relayed = jnp.logical_and(has_crs, jnp.logical_not(turn))
    par = {"seq": s, "ch": o}
    sib = {"seq": sib_s, "ch": g}
    crs = {"seq": crs_s, "ch": g}
    dcr = {"seq": crs_s, "ch": o}
    dsb = {"seq": sib_s, "ch": o}
    cut = {"seq": cut_s, "ch": o}
    x_bit = lax.rem(s // 2, 2)
    x_pair = s + 2 - 4 * x_bit
    mates = [{"seq": x_pair + z_step, "ch": g}, {"seq": x_pair, "ch": g}, {"seq": s + z_step, "ch": g}]
    partners = [par, sib, cut] + mates
    middle = s // 2 == seq_devices // 4

    barrier = pltpu.get_barrier_semaphore()
    for device in partners:
        pl.semaphore_signal(barrier, inc=1, device_id=device, device_id_type=MESH)

    back = [{"seq": lax.rem(s + seq_devices - 2, seq_devices), "ch": ch} for ch in (g, o)]
    fed = [{"seq": lax.rem(s + 2, seq_devices), "ch": ch} for ch in (g, o)]
    for device, when in ((crs, has_crs), (dcr, direct), (dsb, middle), (back[0], ahead), (back[1], ahead)):
        pl.when(when)(functools.partial(
            pl.semaphore_signal, barrier, inc=1, device_id=device, device_id_type=MESH
        ))

    local = []

    def fetch(src, dst):
        copy = pltpu.make_async_copy(src, dst, local_sem.at[len(local)])
        copy.start()
        local.append(copy)
        return copy

    def fetch_pair(first_src, second_src, dst):
        both_here = pltpu.make_async_copy(dst, dst, local_sem.at[len(local)])
        for k, src in enumerate((first_src, second_src)):
            pltpu.make_async_copy(src, dst.at[k], local_sem.at[len(local)]).start()
        local.append(both_here)

    own_copy = fetch(stream, xr.at[g, 1])
    fetch_pair(norm_gain, norm_shift, norms)
    fetch_pair(mid_gain, mid_shift, mids)
    cw0_copy = fetch(conv_weight.at[0], cw.at[0])
    mw0_copy = fetch(mix_weight.at[0], mw.at[0, g])
    cw1_copy = fetch(conv_weight.at[1], cw.at[1])
    mw1_copy = fetch(mix_weight.at[1], mw.at[1, g])
    up_copies = [fetch(up_weight, uw), fetch(skip, skipb)]
    fetch_pair(up_gain, up_shift, ups)
    ng, ns, mg, ms, ug, us = norms.at[0], norms.at[1], mids.at[0], mids.at[1], ups.at[0], ups.at[1]

    sends = []
    names = {}

    def landing(name):
        return recv_sem.at[names.setdefault(name, len(names))]

    def send(name, src, dst, device, when=None, start=None):
        copy = pltpu.make_async_remote_copy(
            src_ref=src, dst_ref=dst, send_sem=send_sem.at[0], recv_sem=landing(name),
            device_id=device, device_id_type=MESH,
        )
        sends.append((copy, when))
        if when is None:
            copy.start()
        else:
            pl.when(when if start is None else start)(copy.start)
        return copy

    def arrive(name, block):
        pltpu.make_async_remote_copy(
            src_ref=block, dst_ref=block, send_sem=send_sem.at[0], recv_sem=landing(name),
            device_id=par, device_id_type=MESH,
        ).wait_recv()

    def arrive_if(when, name, block):
        pl.when(when)(functools.partial(arrive, name, block))

    def weights(name, n, rows, device):
        return send(name, mw.at[n, o, rows], mw.at[n, o, rows], device)

    def drain():
        for copy, when in sends:
            if when is None:
                copy.wait_send()
        for group in (has_crs, direct, relayed, ahead, crs_edges, direct_edges, feeder):
            some = [copy for copy, when in sends if when is group]

            @pl.when(group)
            def _():
                for copy in some:
                    copy.wait_send()

    to_sib = my_sib = 0
    to_crs = my_crs = 2
    sib_side = 2 - 2 * core
    crs_side = 2 * core
    near = pl.ds(pl.multiple_of(32 * core, 32), 32)
    far = pl.ds(pl.multiple_of(32 - 32 * core, 32), 32)

    def piece(x, z):
        return pl.ds(pl.multiple_of(128 * core + 32 * x + 64 * z, 32), 32)

    theirs = pl.ds(pl.multiple_of(128 - 128 * core, 128), 128)
    pieces = [piece(x_bit, z_bit), piece(1 - x_bit, 1 - z_bit), piece(1 - x_bit, z_bit), piece(x_bit, 1 - z_bit)]

    own_copy.wait()
    entered = len(partners) + has_crs.astype(jnp.int32) + direct.astype(jnp.int32) + middle.astype(jnp.int32)
    entered = entered + 2 * feeder.astype(jnp.int32)

    @pl.when(jnp.logical_not(ahead))
    def _():
        pl.semaphore_wait(barrier, entered)

    @pl.when(s == 0)
    def _():
        pl.semaphore_signal(go_sem, inc=1, device_id=cut, device_id_type=MESH)

    @pl.when(s == seq_devices // 2 + 1)
    def _():
        pl.semaphore_signal(go_sem, inc=1, device_id=sib, device_id_type=MESH)

    @pl.when(ahead)
    def _():
        pl.semaphore_wait(go_sem, 2)

    def vouch():
        pl.semaphore_signal(known_sem, inc=1, device_id=sib, device_id_type=MESH)
        pl.when(has_crs)(functools.partial(
            pl.semaphore_signal, known_sem, inc=1, device_id=crs, device_id_type=MESH
        ))

    pl.when(jnp.logical_not(ahead))(vouch)

    for b in range(2):
        send(f"x_par{b}", xr.at[g, 1, b, near], xr.at[g, 1, b, near], par)
    x_crs = send("x_crs", xr.at[g, 1, :, near], xr.at[g, to_crs, :, near], crs, has_crs, at_once)
    x_dcr = send("x_near", xr.at[g, 1, :, near], xr.at[g, to_crs, :, near], dcr, direct, jnp.logical_and(direct, at_once))
    send("w_cut0", mix_weight.at[0, pieces[0]], mw.at[0, g, pieces[0]], cut)
    send("x_par2", xr.at[g, 1, :, far], xr.at[g, 1, :, far], par)
    send("x_sib", xr.at[g, 1], xr.at[g, to_sib], sib)
    x_crs2 = send("x_far", xr.at[g, 1, :, far], xr.at[g, to_crs, :, far], crs, has_crs, at_once)
    for device in fed:
        send("x_feed", xr.at[g, 1, :, pl.ds(48, 16)], ex.at[g], device, feeder)

    def activate0(gg, slot, rows, dst_row, valid):
        cols = pl.ds(pl.multiple_of(gg * 512, 512), 512)
        gain = ng[0:1, cols]
        shift = ns[0:1, cols]
        for b in range(2):
            v = gelu(xr[gg, slot, b, rows, :].astype(F32) * gain + shift)
            if valid is not None:
                v = jnp.where(valid, v, 0.0)
            a0[gg, b, dst_row, :] = v.astype(BF16)

    def conv0(gg):
        acc = None
        for k in range(3):
            term = dot(
                a0[gg, :, 32 * k : 32 * k + ROWS, :].reshape(128, 512),
                cw[0, k, pl.ds(pl.multiple_of(gg * 512, 512), 512), :],
            )
            acc = term if acc is None else acc + term
        return acc

    sib_src = pl.ds(pl.multiple_of(32 * core, 32), 32)
    crs_src = pl.ds(pl.multiple_of(32 - 32 * core, 32), 32)
    sib_dst = pl.ds(pl.multiple_of(96 - 96 * core, 32), 32)
    crs_dst = pl.ds(pl.multiple_of(96 * core, 32), 32)
    whole = pl.ds(0, ROWS)
    centre = pl.ds(32, ROWS)

    for copy in local[1:3]:
        copy.wait()
    activate0(g, 1, whole, centre, None)
    arrive("x_sib", xr.at[g, my_sib])
    activate0(g, my_sib, sib_src, sib_dst, None)
    arrive_if(in_turn, "x_crs", xr.at[g, my_crs, :, far])

    @pl.when(in_turn)
    def _():
        activate0(g, my_crs, crs_src, crs_dst, None)

    @pl.when(jnp.logical_not(in_turn))
    def _():
        a0[g, :, crs_dst, :] = jnp.zeros((2, 32, 512), BF16)

    @pl.when(ahead)
    def _():
        pl.semaphore_wait(barrier, entered)
        x_crs.start()
        x_dcr.start()

    for b in range(2):
        arrive(f"x_par{b}", xr.at[o, 1, b, near])
        send("x_near", xr.at[o, 1, b, near], xr.at[o, to_crs, b, near], crs, relayed)
    cw0_copy.wait()
    accf[...] = conv0(g)
    arrive("x_par2", xr.at[o, 1, :, far])
    send("x_fwd", xr.at[o, 1, :, far], xr.at[o, to_sib, :, far], sib)
    send("w_cut1", mix_weight.at[1, pieces[0]], mw.at[1, g, pieces[0]], cut)
    activate0(o, 1, whole, centre, None)
    arrive("w_cut0", mw.at[0, o, pieces[0]])
    for m in range(3):
        weights(f"w_mate{m}", 0, pieces[0], mates[m])
    weights("w_fwd0", 0, pieces[0], sib)
    send("x_far", xr.at[o, 1, :, far], xr.at[o, to_crs, :, far], crs, has_crs)
    send("x_fwd2", xr.at[o, 1, :, near], xr.at[o, to_sib, :, near], sib)
    arrive("x_fwd", xr.at[o, my_sib, :, near])
    activate0(o, my_sib, sib_src, sib_dst, None)

    pl.when(ahead)(x_crs2.start)
    pl.when(ahead)(vouch)

    @pl.when(seam)
    def _():
        arrive("x_crs", xr.at[g, my_crs, :, far])
        activate0(g, my_crs, crs_src, crs_dst, None)
        accf[...] = conv0(g)

    arrive_if(has_crs, "x_near", xr.at[o, my_crs, :, far])
    activate0(o, my_crs, crs_src, crs_dst, has_crs)
    acc = accf[...] + conv0(o)
    hb[g, 1] = gelu(acc * mg[0:1, :] + ms[0:1, :]).astype(BF16)

    halves = [pl.ds(ROWS * b, ROWS) for b in range(2)]
    for b in range(2):
        send(f"h_crs{b}", hb.at[g, 1, halves[b]], hb.at[g, to_crs, halves[b]], dcr, direct)
    for b in range(2):
        send(f"h_par{b}", hb.at[g, 1, halves[b]], hb.at[g, 1, halves[b]], par)
    for b in range(2):
        send(f"h_crs{b}", hb.at[g, 1, halves[b]], hb.at[g, to_crs, halves[b]], crs, has_crs)
    send("h_sib", hb.at[g, 1], hb.at[g, to_sib], sib)
    for device in fed:
        for b in range(2):
            send("h_feed", hb.at[g, 1, pl.ds(ROWS * b + 48, 16)], eg.at[g, pl.ds(16 * b, 16)], device, feeder)
    for m in range(3):
        arrive(f"w_mate{m}", mw.at[0, o, pieces[m + 1]])
        weights("w_fwd0", 0, pieces[m + 1], sib)

    def mix0(slot, tap, valid, rows, batch):
        count = rows.stop - rows.start
        for n in range(4):
            cols = slice(256 * n, 256 * n + 256)
            gg, inner = n // 2, slice(256 * (n % 2), 256 * (n % 2) + 256)
            z = dot(hb[0, slot, rows], mw[0, 0, :, cols]) + dot(hb[1, slot, rows], mw[0, 1, :, cols])
            x = xr[gg, slot, batch, :, inner].reshape(count, 256).astype(F32) + z
            x = x.astype(BF16)
            x1[slot, rows, cols] = x
            v = gelu(x.astype(F32) * ng[1:2, cols] + ns[1:2, cols])
            if valid is not None:
                v = jnp.where(valid, v, 0.0)
            a1[slot, rows, cols] = v.astype(BF16)
        return dot(a1[slot, rows], cw[1, tap])

    last = pl.ds(pl.multiple_of(48 - 48 * core, 16), 16)
    first = pl.ds(pl.multiple_of(48 * core, 16), 16)
    every = slice(0, 128)
    both = slice(0, 2)
    mw0_copy.wait()
    cw1_copy.wait()
    for b in range(2):
        arrive(f"h_par{b}", hb.at[o, 1, halves[b]])
        send(f"h_crs{b}", hb.at[o, 1, halves[b]], hb.at[o, to_crs, halves[b]], crs, relayed)
        send("h_sib", hb.at[o, 1, halves[b]], hb.at[o, to_sib, halves[b]], sib)
    arrive("w_cut1", mw.at[1, o, pieces[0]])
    for m in range(3):
        weights(f"w_mate{m + 3}", 1, pieces[0], mates[m])
    weights("w_fwd1", 1, pieces[0], sib)
    arrive("w_fwd0", mw.at[0, o, theirs])
    acc = mix0(1, 1, None, every, both)
    arrive("h_sib", hb.at[:, my_sib])
    arrive("x_fwd2", xr.at[o, my_sib, :, far])
    acc = acc + mix0(my_sib, sib_side, None, every, both)
    arrive_if(has_crs, "x_far", xr.at[:, my_crs, :, near])
    for b in range(2):
        rows = slice(ROWS * b, ROWS * b + ROWS)
        arrive_if(has_crs, f"h_crs{b}", hb.at[:, my_crs, rows])
        part = acc[rows] + mix0(my_crs, crs_side, has_crs, rows, slice(b, b + 1))
        h1[g, b] = gelu(part * mg[1:2, :] + ms[1:2, :]).astype(BF16)
        if b == 1:
            send("x_crs", h1.at[g, :, first], eh.at[g, 1 - core], dcr, direct_edges)
        send(f"x_par{b}", h1.at[g, b], h1.at[g, b], par)

    pl.semaphore_wait(known_sem, 1 + has_crs.astype(jnp.int32))
    send("x_crs", h1.at[g, :, first], eh.at[g, 1 - core], crs, crs_edges)
    send("x_crs", h1.at[g, :, first], eh.at[g, 1 - core], dcr, relayed)
    send("x_sib", h1.at[g, :, last], eh.at[g, core], dsb)
    send("x_sib", h1.at[g, :, last], eh.at[g, core], sib)

    def edge_behind():
        arrive("x_feed", ex)
        arrive("h_feed", eg)
        for n in range(4):
            cols = slice(256 * n, 256 * n + 256)
            gg, inner = n // 2, slice(256 * (n % 2), 256 * (n % 2) + 256)
            z = dot(eg[0], mw[0, 0, :, cols]) + dot(eg[1], mw[0, 1, :, cols])
            x = (ex[gg, :, :, inner].reshape(32, 256).astype(F32) + z).astype(BF16).astype(F32)
            ea[:, cols] = gelu(x * ng[1:2, cols] + ns[1:2, cols]).astype(BF16)
        y = dot(ea[...], cw[1, 0])
        for k in range(2):
            tail = jnp.concatenate([a1[2 - k, ROWS * b + 48 : ROWS * b + ROWS, :] for b in range(2)], axis=0)
            y = y + dot(tail, cw[1, k + 1])
        eh[g, 0] = gelu(y * mg[1:2, :] + ms[1:2, :]).astype(BF16).reshape(2, 16, 256)

    pl.when(ahead)(edge_behind)
    send("x_crs", eh.at[g, 0], eh.at[g, 0], par, ahead)

    mw1_copy.wait()
    for copy in up_copies + local[-1:]:
        copy.wait()

    def half_top():
        for n in range(4):
            cols = slice(256 * n, 256 * n + 256)
            zf[:, cols] = dot(h1[g].reshape(128, 256), mw[1, g, :, cols]) + x1[1, :, cols].astype(F32)

    def whole_top(b):
        rows = slice(ROWS * b, ROWS * b + ROWS)
        for n in range(4):
            cols = slice(256 * n, 256 * n + 256)
            v = (zf[rows, cols] + dot(h1[o, b], mw[1, o, :, cols])).astype(BF16).astype(F32)
            v = gelu(v * ug[0:1, cols] + us[0:1, cols])
            uf[b, 8 : 8 + ROWS, cols] = v.astype(BF16).astype(F32)

    def edge_top():
        left, right = 2 - 2 * core, 2 * core
        for n in range(4):
            cols = slice(256 * n, 256 * n + 256)
            z = dot(eh[0].reshape(64, 256), mw[1, 0, :, cols]) + dot(eh[1].reshape(64, 256), mw[1, 1, :, cols])
            for b in range(2):
                for base, part, valid, to in (
                    (x1[left, ROWS * b + 48 : ROWS * b + ROWS, cols].astype(F32)[8:], z[16 * b + 8 : 16 * b + 16],
                     s > 0, slice(0, 8)),
                    (x1[right, ROWS * b : ROWS * b + 16, cols].astype(F32)[:8], z[32 + 16 * b : 40 + 16 * b],
                     s < seq_devices - 1, slice(8 + ROWS, 16 + ROWS)),
                ):
                    v = (base + part).astype(BF16).astype(F32)
                    v = gelu(v * ug[0:1, cols] + us[0:1, cols]).astype(BF16).astype(F32)
                    uf[b, to, cols] = jnp.where(valid, v, 0.0)

    def rows_at(offset):
        return jnp.concatenate(
            [uf[b, 8 + offset : 8 + offset + ROWS, :].astype(BF16) for b in range(2)], axis=0
        )

    def centre_taps():
        here = rows_at(0)
        for r in range(4):
            cf[r] = dot(here, uw[2 + r])

    def outer_taps():
        for r in range(4):
            v = cf[r] + (dot(rows_at(-1), uw[6 + r]) if r < 2 else dot(rows_at(1), uw[r - 2]))
            for b in range(2):
                for half in range(2):
                    outf[b, half, pl.ds(r, ROWS, stride=4), :] = v[
                        ROWS * b : ROWS * b + ROWS, 128 * half : 128 * half + 128
                    ]

    def finish():
        for half in range(2):
            lanes = slice(128 * half, 128 * half + 128)
            out[:, :, lanes] = (outf[:, half] + skipb[:, :, lanes].astype(F32)).astype(BF16)

    for m in range(3):
        arrive(f"w_mate{m + 3}", mw.at[1, o, pieces[m + 1]])
        weights("w_fwd1", 1, pieces[m + 1], sib)
    half_top()
    arrive("w_fwd1", mw.at[1, o, theirs])
    for b in range(2):
        arrive(f"x_par{b}", h1.at[o, b])
        whole_top(b)
    centre_taps()
    arrive("x_sib", eh.at[:, 1 - core])
    arrive_if(at_once, "x_crs", eh.at[:, core])
    arrive_if(ahead, "x_crs", eh.at[o, core])
    edge_top()
    outer_taps()
    finish()
    drain()
    assert len(names) == LANDINGS and len(local) == LOCALS


def body(
    seq_devices, stream, skip, norm_gain, norm_shift, conv_weight, mid_gain, mid_shift, mix_weight, up_gain, up_shift, up_weight
):
    anywhere = pl.BlockSpec(memory_space=pl.ANY)
    return pl.pallas_call(
        functools.partial(kernel, seq_devices),
        name="bottleneck",
        out_shape=pltpu.VMEM((2, 256, 256), BF16),
        in_specs=[anywhere] * 11,
        out_specs=pl.BlockSpec(memory_space=pltpu.VMEM),
        scratch_shapes=[
            pltpu.VMEM((2, 3, 2, 64, 512), BF16),
            pltpu.VMEM((2, 2, 128, 512), BF16),
            pltpu.VMEM((2, 3, 128, 256), BF16),
            pltpu.VMEM((2, 2, 256, 1024), BF16),
            pltpu.VMEM((2, 3, 1024, 256), BF16),
            pltpu.VMEM((8, 1024, 256), BF16),
            pltpu.VMEM((3, 128, 1024), BF16),
            pltpu.VMEM((3, 128, 1024), BF16),
            pltpu.VMEM((2, 2, 64, 256), BF16),
            pltpu.VMEM((2, 2, 2, 16, 256), BF16),
            pltpu.VMEM((2, 2, 16, 512), BF16),
            pltpu.VMEM((2, 32, 256), BF16),
            pltpu.VMEM((32, 1024), BF16),
            pltpu.VMEM((2, 80, 1024), F32),
            pltpu.VMEM((2, 2, 256, 128), F32),
            pltpu.VMEM((128, 1024), F32),
            pltpu.VMEM((4, 128, 256), F32),
            pltpu.VMEM((128, 256), F32),
            pltpu.VMEM((2, 256, 256), BF16),
            pltpu.VMEM((2, 2, 1024), F32),
            pltpu.VMEM((2, 2, 256), F32),
            pltpu.VMEM((2, 1, 1024), F32),
            pltpu.SemaphoreType.DMA((LOCALS,)),
            pltpu.SemaphoreType.DMA((1,)),
            pltpu.SemaphoreType.DMA((LANDINGS,)),
            pltpu.SemaphoreType.REGULAR,
            pltpu.SemaphoreType.REGULAR,
        ],
        compiler_params=pltpu.CompilerParams(
            collective_id=0, has_side_effects=True, vmem_limit_bytes=56 * 1024 * 1024
        ),
    )(
        stream, skip, norm_gain, norm_shift, conv_weight, mid_gain, mid_shift, mix_weight,
        up_gain.reshape(1, -1), up_shift.reshape(1, -1), up_weight,
    )


def solution(mesh):
    placed = (
        P(None, "seq", "ch"),
        P(None, "seq", "ch"),
        P(),
        P(),
        P(None, None, None, "ch"),
        P(None, "ch"),
        P(None, "ch"),
        P(None, "ch", None),
        P(),
        P(),
        P(None, None, "ch"),
    )
    return jax.shard_map(
        functools.partial(body, mesh.shape["seq"]),
        mesh=mesh, in_specs=placed, out_specs=P(None, "seq", "ch"), check_vma=False,
    )
```
